1024 devices in a mesh: tile: 32 (over z_lo, core), spec: 32 (over y, z_hi, x).
Axes of the slice: x: 4, y: 4, z: 32 (z_hi: 2, z_lo: 16; z = z_hi * 16 + z_lo), core: 2. Of those that a mesh axis runs over, the one named last changes fastest.
Arguments:
- object_field: float32 [2, 8192, 512], P(None, 'tile'), may hold values from -5 to 5
- probe_modes: float32 [32, 2, 256, 256], P('spec'), may hold values from -5 to 5
- amplitude: float32 [128, 256, 256], P('tile'), may hold values from 1 to 8
- positions: int32 [128, 2], P('tile'), may hold values from 0 to 256, as said below
Outputs:
- updated_object: float32 [2, 8192, 512], P(None, ('tile', 'spec'))
The draws below stay inside these ranges and needn't reach their ends.
Inputs may be any that keep to these rules, and one draw needn't show every extreme that they name: positions[j, 0] lies in 0 to 255 and positions[j, 1] in 0 to 256; both ends of both ranges occur.
All inputs are finite; a program needn't handle non-finite values.
Results may differ from the reference program's by a relative error of at most 0.00005.
Values sent between devices are 32-bit elements; how exact they have to be, the bound alone decides.
No kernel may reach another device: no remote copies, remote signals or barrier semaphores. Data moves between devices by JAX's collectives and lax.ppermute only.
A program may use at most 32 MiB of HBM per device.

```python
import math
import jax
import jax.numpy as jnp
from jax import lax

PROBE = 256
STRIP = 256
WIDTH = 512
POS_DEV = 4
MODES = 32
PATTERNS = 128
OBJ_ROWS = 8192


def draw_positions(key, part):
    key = jax.random.fold_in(key, 11)
    row_key, col_key = jax.random.split(key)
    row_offsets = jax.random.randint(row_key, (PATTERNS,), 0, STRIP)
    col_offsets = jax.random.randint(col_key, (PATTERNS,), 0, WIDTH - PROBE + 1)
    row_offsets = row_offsets.at[0].set(STRIP - 1).at[1].set(0)
    col_offsets = col_offsets.at[0].set(0).at[1].set(WIDTH - PROBE)
    return jnp.stack([row_offsets, col_offsets], 1).astype(jnp.int32)


def block_levels(own_key, shape, cuts, least, largest):
    level, own = 1.0, jax.random.fold_in(own_key, 6)
    for dim, blocks in cuts:
        heights = jnp.exp(jax.random.uniform(jax.random.fold_in(own, dim), (blocks,), jnp.float32, least / len(cuts), largest / len(cuts)))
        level = level * jnp.repeat(heights, shape[dim] // blocks).reshape([-1 if axis == dim else 1 for axis in range(len(shape))])
    return level


def scatter_about(key, shape, width, bound, shards=(), held_as=jnp.bfloat16):
    loudness = block_levels(key, shape, shards, -0.22, 0.18) if shards else 1.0
    values = jax.random.normal(key, shape, jnp.float32) * width * loudness
    return jnp.minimum(jnp.maximum(values, -bound), bound).astype(held_as)


def setup_inputs(seed: int = 0) -> dict:
    arg_keys = jax.random.split(jax.random.key(seed), 5)
    object_field = scatter_about(arg_keys[0], (2, OBJ_ROWS, WIDTH), 0.7, 5.0, ((1, 32),), jnp.float32)
    probe_modes = scatter_about(arg_keys[1], (MODES, 2, PROBE, PROBE), 0.7, 5.0, ((0, 32),), jnp.float32)
    amplitude = jnp.clip(jnp.exp(math.log(8.0) - 2.0794415 * jax.random.uniform(arg_keys[2], (PATTERNS, PROBE, PROBE), jnp.float32) ** block_levels(arg_keys[2], (PATTERNS, PROBE, PROBE), ((0, 32),), -0.2, 0.2)), 1.0, 8.0)
    positions = draw_positions(jax.random.fold_in(arg_keys[4], 71), 0)
    return {"object_field": object_field, "probe_modes": probe_modes, "amplitude": amplitude, "positions": positions}


def reference(object_field, probe_modes, amplitude, positions):
    field = object_field[0] + 1j * object_field[1]
    extended = jnp.concatenate([field, field[:STRIP]], 0)
    modes_complex = probe_modes[:, 0] + 1j * probe_modes[:, 1]
    tile_of = (jnp.arange(PATTERNS) // POS_DEV).astype(jnp.int32)
    global_rows = (tile_of * STRIP + positions[:, 0]).astype(jnp.int32)
    columns = positions[:, 1].astype(jnp.int32)

    def one_pattern(inputs):
        row_start, col_start, measured = inputs
        patch = lax.dynamic_slice(extended, (row_start, col_start), (PROBE, PROBE))
        exit_wave = modes_complex * patch
        far = jnp.fft.fft2(exit_wave, axes=(-2, -1), norm='ortho')
        intensity = lax.optimization_barrier(jnp.sum(jnp.real(far) ** 2 + jnp.imag(far) ** 2, 0))
        scaling = measured / jnp.sqrt(intensity + 0.05 * MODES)
        revised = jnp.fft.ifft2(far * scaling, axes=(-2, -1), norm='ortho')
        return lax.optimization_barrier(jnp.sum(jnp.conj(modes_complex) * (revised - exit_wave), 0))
    contributions = lax.map(one_pattern, (global_rows, columns, amplitude))

    def accumulate(pattern, gradient):
        row_start = global_rows[pattern]
        col_start = columns[pattern]
        current = lax.dynamic_slice(gradient, (row_start, col_start), (PROBE, PROBE))
        return lax.dynamic_update_slice(gradient, current + contributions[pattern], (row_start, col_start))
    gradient = lax.fori_loop(0, PATTERNS, accumulate, jnp.zeros(extended.shape, extended.dtype))
    folded = gradient[:OBJ_ROWS].at[:STRIP].add(gradient[OBJ_ROWS:])
    updated = field + 0.5 * folded / MODES
    return jnp.stack([jnp.real(updated), jnp.imag(updated)]).astype(jnp.float32)
```

```python
import math

import jax
import jax.numpy as jnp
import ml_dtypes
import numpy as np
from jax import lax
from jax.experimental import pallas as pl
from jax.experimental.pallas import tpu as pltpu
from jax.sharding import Mesh, PartitionSpec as P

AXES = ("zlo", "core", "y", "zhi", "x")
SIZES = (16, 2, 4, 2, 4)
PLANE = ("y", "x")
SIDE = 256
PLANE_SIZE = 16
SPAN = SIDE + 8


def pairs_of(move):
    count = math.prod(SIZES)
    pairs = []
    for source in range(count):
        place = np.unravel_index(source, SIZES)
        target = np.ravel_multi_index(move(*(int(v) for v in place)), SIZES)
        pairs.append((source, int(target)))
    return pairs


def along_ring(steps):
    def move(zlo, core, y, zhi, x):
        chip, core = divmod(((zhi * 16 + zlo) * 2 + core + steps) % 64, 2)
        return chip % 16, core, y, chip // 16, x

    return move


def other_half(zlo, core, y, zhi, x):
    return zlo, core, y, 1 - zhi, x


def moved(value, move):
    return lax.ppermute(value, AXES, pairs_of(move))


def tables():
    index = np.arange(SIDE)
    angle = (np.outer(index, index) % SIDE) * (2.0 * math.pi / SIDE)
    cos, sin = np.cos(angle) / 16.0, np.sin(angle) / 16.0
    forward = np.block([[cos, sin], [-sin, cos]])
    out = []
    for table in (forward, forward.T):
        high = table.astype(np.float32).astype(ml_dtypes.bfloat16)
        low = (table - high.astype(np.float64)).astype(np.float32)
        out += [high, low.astype(ml_dtypes.bfloat16)]
    return out


def halves(value):
    high = value.astype(jnp.bfloat16)
    return high, (value - high.astype(jnp.float32)).astype(jnp.bfloat16)


def product(a_high, a_low, b_high, b_low):
    dot = lambda a, b: jnp.dot(a, b, preferred_element_type=jnp.float32)
    return dot(a_high, b_high) + (dot(a_high, b_low) + dot(a_low, b_high))


def transform(real, imag, left, right):
    high, low = halves(jnp.concatenate([real, imag], 0))
    part = product(left[0][...], left[1][...], high, low)
    high, low = halves(jnp.concatenate([part[:SIDE], part[SIDE:]], 1))
    out = product(high, low, right[0][...], right[1][...])
    return out[:, :SIDE], out[:, SIDE:]


def forward_kernel(pos, own, halo, probe, fh, fl, ih, il, far, intensity, ext):
    ext[:, :SIDE] = own[...]
    ext[:, SIDE:] = halo[...]

    def pattern(p, carry):
        row, col = pos[p, 0], pos[p, 1]
        base = pl.multiple_of(row // 8 * 8, 8)
        left = lax.rem(512 - col, 512)
        up = lax.rem(SPAN - (row - base), SPAN)

        def window(part):
            rows = pltpu.roll(ext[part, pl.ds(base, SPAN), :], left, 1)[:, :SIDE]
            return pltpu.roll(rows, up, 0)[:SIDE]

        patch_re, patch_im = window(0), window(1)
        probe_re, probe_im = probe[0], probe[1]
        exit_re = probe_re * patch_re - probe_im * patch_im
        exit_im = probe_re * patch_im + probe_im * patch_re
        far_re, far_im = transform(exit_re, exit_im, (fh, fl), (ih, il))
        far[p, 0] = far_re
        far[p, 1] = far_im
        strength = far_re * far_re + far_im * far_im
        intensity[:, p] = strength.reshape(PLANE_SIZE, SIDE // PLANE_SIZE, SIDE)
        return carry

    lax.fori_loop(0, pos.shape[0], pattern, 0)


def inverse_kernel(pos, change, far, probe, fh, fl, ih, il, out, grad):
    grad[...] = jnp.zeros_like(grad)

    def pattern(p, carry):
        row, col = pos[p, 0], pos[p, 1]
        factor = change[:, p].reshape(SIDE, SIDE)
        diff_re, diff_im = transform(far[p, 0] * factor, far[p, 1] * factor, (ih, il), (fh, fl))
        probe_re, probe_im = probe[0], probe[1]
        add_re = probe_re * diff_re + probe_im * diff_im
        add_im = probe_re * diff_im - probe_im * diff_re
        base = pl.multiple_of(row // 8 * 8, 8)
        below = jnp.zeros((SPAN - SIDE, SIDE), jnp.float32)
        beside = jnp.zeros((SPAN, SIDE), jnp.float32)
        for part, add in ((0, add_re), (1, add_im)):
            placed = pltpu.roll(jnp.concatenate([add, below], 0), row - base, 0)
            placed = pltpu.roll(jnp.concatenate([placed, beside], 1), col, 1)
            grad[part, pl.ds(base, SPAN), :] += placed
        return carry

    lax.fori_loop(0, pos.shape[0], pattern, 0)
    for d in range(PLANE_SIZE):
        for lower in range(2):
            for half in range(2):
                start = lower * SIDE + (d // 4) * 64 + half * 32 + (d % 4) * 8
                out[d, lower, :, half] = grad[:, start : start + 8, :]


VMEM = pl.BlockSpec(memory_space=pltpu.VMEM)
SMEM = pl.BlockSpec(memory_space=pltpu.SMEM)
PARAMS = pltpu.CompilerParams(vmem_limit_bytes=40 * 1024 * 1024)


def forward(positions, own, halo, probe, table):
    count = positions.shape[0]
    return pl.pallas_call(
        forward_kernel,
        out_shape=(
            jax.ShapeDtypeStruct((count, 2, SIDE, SIDE), jnp.float32),
            jax.ShapeDtypeStruct((PLANE_SIZE, count, SIDE // PLANE_SIZE, SIDE), jnp.float32),
        ),
        in_specs=[SMEM] + [VMEM] * 7,
        out_specs=(VMEM, VMEM),
        scratch_shapes=[pltpu.VMEM((2, 512, 512), jnp.float32)],
        compiler_params=PARAMS,
        name="forward",
    )(positions, own, halo, probe, *table)


def inverse(positions, change, far, probe, table):
    return pl.pallas_call(
        inverse_kernel,
        out_shape=jax.ShapeDtypeStruct((PLANE_SIZE, 2, 2, 2, 8, 512), jnp.float32),
        in_specs=[SMEM] + [VMEM] * 7,
        out_specs=VMEM,
        scratch_shapes=[pltpu.VMEM((2, 512, 512), jnp.float32)],
        compiler_params=PARAMS,
        name="inverse",
    )(positions, change, far, probe, *table)


def body(object_field, probe_modes, amplitude, positions):
    modes = 32
    table = [jnp.asarray(t) for t in tables()]
    probe = probe_modes[0]
    halo = moved(object_field, along_ring(-1))
    far, intensity = forward(positions, object_field, halo, probe, table)

    mine = lax.axis_index("y") * 4 + lax.axis_index("x")
    rows = SIDE // PLANE_SIZE
    summed = jnp.sum(lax.all_to_all(intensity, PLANE, 0, 0), 0)
    summed = summed + moved(summed, other_half)
    measured = lax.dynamic_slice_in_dim(amplitude, mine * rows, rows, 1)
    change = measured / jnp.sqrt(summed + 0.05 * modes) - 1.0
    change = jnp.broadcast_to(change[None], intensity.shape)
    change = lax.all_to_all(change, PLANE, 0, 0)

    gradient = inverse(positions, change, far, probe, table)
    gradient = jnp.sum(lax.all_to_all(gradient, PLANE, 0, 0), 0)
    total = gradient[0] + moved(gradient[1], along_ring(1))
    half = lax.axis_index("zhi")
    kept = lax.dynamic_index_in_dim(total, half, 1, keepdims=False)
    sent = lax.dynamic_index_in_dim(total, 1 - half, 1, keepdims=False)
    total = kept + moved(sent, other_half)
    place = (lax.axis_index("y") * 2 + half) * 4 + lax.axis_index("x")
    own = lax.dynamic_slice_in_dim(object_field, place * 8, 8, 1)
    return own + 0.5 * total / modes


def solution(mesh):
    fine = Mesh(mesh.devices.reshape(SIZES), AXES)
    tile, spec = ("zlo", "core"), ("y", "zhi", "x")
    placed = (
        P(None, tile, None),
        P(spec, None, None, None),
        P(tile, None, None),
        P(tile, None),
    )
    return jax.shard_map(
        body, mesh=fine, in_specs=placed, out_specs=P(None, tile + spec, None), check_vma=False
    )
```

```python
import math

import jax
import jax.numpy as jnp
import ml_dtypes
import numpy as np
from jax import lax
from jax.experimental import pallas as pl
from jax.experimental.pallas import tpu as pltpu
from jax.sharding import Mesh, PartitionSpec as P

AXES = ("zlo", "core", "y", "zhi", "x")
SIZES = (16, 2, 4, 2, 4)
PLANE = ("y", "x")
SIDE = 256
HALF = SIDE // 2
WIDTH = 512
COUNT = 4
MODES = 32
PLANE_SIZE = 16
ROWS = SIDE // PLANE_SIZE
SPAN = SIDE + 8


def pairs_of(move):
    count = math.prod(SIZES)
    pairs = []
    for source in range(count):
        place = np.unravel_index(source, SIZES)
        target = np.ravel_multi_index(move(*(int(v) for v in place)), SIZES)
        pairs.append((source, int(target)))
    return pairs


def along_ring(steps):
    def move(zlo, core, y, zhi, x):
        chip, core = divmod(((zhi * 16 + zlo) * 2 + core + steps) % 64, 2)
        return chip % 16, core, y, chip // 16, x

    return move


def other_core(zlo, core, y, zhi, x):
    return zlo, 1 - core, y, zhi, x


def moved(value, move):
    return lax.ppermute(value, AXES, pairs_of(move))


def tables():
    out = np.zeros((2, 2, 2, SIDE, SIDE), ml_dtypes.bfloat16)
    for parity in range(2):
        freq = 2 * np.arange(HALF) + parity
        angle = (np.outer(freq, np.arange(HALF)) % SIDE) * (2.0 * math.pi / SIDE)
        cos, sin = np.cos(angle) / 16.0, np.sin(angle) / 16.0
        whole = np.block([[cos, sin], [-sin, cos]])
        for turned, table in enumerate((whole, whole.T)):
            high = table.astype(np.float32).astype(ml_dtypes.bfloat16)
            low = (table - high.astype(np.float64)).astype(np.float32)
            out[turned, parity, 0] = high
            out[turned, parity, 1] = low.astype(ml_dtypes.bfloat16)
    return out


def halves(value):
    high = value.astype(jnp.bfloat16)
    return high, (value - high.astype(jnp.float32)).astype(jnp.bfloat16)


def dot(a, b):
    return jnp.dot(a, b, preferred_element_type=jnp.float32)


def product(a, b):
    return dot(a[0], b[0]) + (dot(a[0], b[1]) + dot(a[1], b[0]))


def side_by_side(*parts):
    return jnp.concatenate(parts, 1)


def stacked(*parts):
    return jnp.concatenate(parts, 0)


def own_share(amp, plane):
    out_row = lax.broadcasted_iota(jnp.int32, (COUNT * ROWS, COUNT * 2 * ROWS), 0)
    in_row = lax.broadcasted_iota(jnp.int32, (COUNT * ROWS, COUNT * 2 * ROWS), 1)
    take_rows = jnp.where(in_row == 2 * out_row + plane // 8, 1.0, 0.0).astype(jnp.bfloat16)
    in_col = lax.broadcasted_iota(jnp.int32, (SIDE, SIDE), 0)
    out_col = lax.broadcasted_iota(jnp.int32, (SIDE, SIDE), 1)
    wanted = jnp.where(out_col < HALF, 2 * out_col, 2 * out_col - (SIDE - 1))
    take_cols = jnp.where(in_col == wanted, 1.0, 0.0).astype(jnp.bfloat16)
    value, total = amp.reshape(COUNT * 2 * ROWS, SIDE), 0.0
    for _ in range(3):
        part = value.astype(jnp.bfloat16)
        value = value - part.astype(jnp.float32)
        total = total + dot(dot(take_rows, part).astype(jnp.bfloat16), take_cols)
    return total.reshape(COUNT, ROWS, SIDE)


def forward_kernel(
    pos, flags, own_hbm, halo_hbm, probe_hbm, gathered_hbm, swapped_hbm, amp_hbm, table_hbm,
    far, intensity, measured, probes, ext, other, swap, amp, table, sems,
):
    core, zhi, plane = flags[0], flags[1], flags[2]
    start = pl.multiple_of(lax.rem(plane, 8) * 2 * ROWS, 2 * ROWS)
    ends = (
        (amp_hbm.at[:, pl.ds(start, 2 * ROWS)], amp),
        (own_hbm, ext.at[:, pl.ds(0, SIDE)]),
        (halo_hbm, ext.at[:, pl.ds(SIDE, SIDE)]),
        (probe_hbm, probes.at[0]),
        (gathered_hbm.at[1 - zhi], other),
        (swapped_hbm, swap),
        (table_hbm, table),
    )
    copies = [pltpu.make_async_copy(*pair, sems.at[i]) for i, pair in enumerate(ends)]
    for copy in copies:
        copy.start()
    copies[0].wait()
    measured[...] = own_share(amp[...], plane)
    for copy in copies[1:]:
        copy.wait()
    probes[1, 0] = jnp.where(core == 0, other[...], swap[...])
    probes[1, 1] = jnp.where(core == 0, swap[...], other[...])

    def times(turned, parity):
        return table[turned, parity, 0], table[turned, parity, 1]

    def pattern(p, carry):
        row, col = pos[p, 0], pos[p, 1]
        base = pl.multiple_of(row // 8 * 8, 8)
        left = lax.rem(WIDTH - col, WIDTH)
        up = lax.rem(SPAN - (row - base), SPAN)

        def window(part):
            rows = pltpu.roll(ext[part, pl.ds(base, SPAN), :], left, 1)[:, :SIDE]
            return pltpu.roll(rows, up, 0)[:SIDE]

        patch_re, patch_im = window(0), window(1)
        sums, differences = [], []
        for m in range(2):
            wave_re = probes[m, 0] * patch_re - probes[m, 1] * patch_im
            wave_im = probes[m, 0] * patch_im + probes[m, 1] * patch_re
            sums.append(stacked(wave_re[:HALF] + wave_re[HALF:], wave_im[:HALF] + wave_im[HALF:]))
            differences.append(
                stacked(wave_re[:HALF] - wave_re[HALF:], wave_im[:HALF] - wave_im[HALF:])
            )
        even = product(times(0, 0), halves(side_by_side(*sums)))
        odd = product(times(0, 1), halves(side_by_side(*differences)))
        sums, differences = [], []
        for m in range(2):
            near, away = slice(m * SIDE, m * SIDE + HALF), slice(m * SIDE + HALF, (m + 1) * SIDE)
            plus = [part[:, near] + part[:, away] for part in (even, odd)]
            minus = [part[:, near] - part[:, away] for part in (even, odd)]
            for kept, parts in ((sums, plus), (differences, minus)):
                kept += [side_by_side(part[:HALF], part[HALF:]) for part in parts]
        for parity, parts in ((0, sums), (1, differences)):
            out = product(halves(stacked(*parts)), times(1, parity))
            far[p, parity] = out
            strength = out[:, :HALF] * out[:, :HALF] + out[:, HALF:] * out[:, HALF:]
            strength = strength[:SIDE] + strength[SIDE:]
            columns = pl.ds(parity * HALF, HALF)
            intensity[:, p, :, columns] = strength.reshape(PLANE_SIZE, ROWS, HALF)
        return carry

    lax.fori_loop(0, COUNT, pattern, 0)


def inverse_kernel(pos, flags, change, far_hbm, probes_hbm, table_hbm, out, grad, far, probes, table, sems):
    ends = ((far_hbm, far), (probes_hbm, probes), (table_hbm, table))
    copies = [pltpu.make_async_copy(*pair, sems.at[i]) for i, pair in enumerate(ends)]
    for copy in copies:
        copy.start()
    grad[...] = jnp.zeros_like(grad)
    for copy in copies:
        copy.wait()

    def times(turned, parity):
        return table[turned, parity, 0], table[turned, parity, 1]

    def pattern(p, carry):
        row, col = pos[p, 0], pos[p, 1]
        factor = change[:, p].reshape(SIDE, SIDE)
        scaled = []
        for parity in range(2):
            half = factor[:, parity * HALF : (parity + 1) * HALF]
            half = stacked(side_by_side(half, half), side_by_side(half, half))
            scaled.append(far[p, parity] * half)
        parts = []
        for parity in range(2):
            blocks = []
            for m in range(2):
                for side in range(2):
                    start = m * SIDE + parity * HALF
                    block = scaled[side][start : start + HALF]
                    blocks.append(stacked(block[:, :HALF], block[:, HALF:]))
            parts.append(product(times(1, parity), halves(side_by_side(*blocks))))
        near, away = parts[0] + parts[1], parts[0] - parts[1]
        parts = []
        for parity in range(2):
            blocks = []
            for m in range(2):
                for rows in (near, away):
                    start = (2 * m + parity) * HALF
                    block = rows[:, start : start + HALF]
                    blocks.append(side_by_side(block[:HALF], block[HALF:]))
            parts.append(product(halves(stacked(*blocks)), times(0, parity)))
        near, away = parts[0] + parts[1], parts[0] - parts[1]
        add_re, add_im = 0.0, 0.0
        for m in range(2):
            rows = slice(m * SIDE, (m + 1) * SIDE)
            diff_re = side_by_side(near[rows, :HALF], away[rows, :HALF])
            diff_im = side_by_side(near[rows, HALF:], away[rows, HALF:])
            add_re += probes[m, 0] * diff_re + probes[m, 1] * diff_im
            add_im += probes[m, 0] * diff_im - probes[m, 1] * diff_re
        base = pl.multiple_of(row // 8 * 8, 8)
        below = jnp.zeros((SPAN - SIDE, SIDE), jnp.float32)
        beside = jnp.zeros((SPAN, WIDTH - SIDE), jnp.float32)
        for part, add in ((0, add_re), (1, add_im)):
            placed = pltpu.roll(stacked(add, below), row - base, 0)
            placed = pltpu.roll(side_by_side(placed, beside), col, 1)
            grad[part, pl.ds(base, SPAN), :] += placed
        return carry

    lax.fori_loop(0, COUNT, pattern, 0)
    for d in range(PLANE_SIZE):
        for lower in range(2):
            start = lower * SIDE + (d // 4) * 64 + flags[1 + 2 * lower] * 32 + (d % 4) * 8
            out[d, lower] = grad[:, pl.ds(pl.multiple_of(start, 8), 8), :]


VMEM = pl.BlockSpec(memory_space=pltpu.VMEM)
SMEM = pl.BlockSpec(memory_space=pltpu.SMEM)
ANY = pl.BlockSpec(memory_space=pl.ANY)
PARAMS = pltpu.CompilerParams(vmem_limit_bytes=44 * 1024 * 1024)
TABLE_VMEM = pltpu.VMEM((2, 2, 2, SIDE, SIDE), jnp.bfloat16)


def floats(*shape):
    return jax.ShapeDtypeStruct(shape, jnp.float32)


def forward(*operands):
    return pl.pallas_call(
        forward_kernel,
        out_shape=(
            floats(COUNT, 2, 2 * SIDE, SIDE),
            floats(PLANE_SIZE, COUNT, ROWS, SIDE),
            floats(COUNT, ROWS, SIDE),
            floats(2, 2, SIDE, SIDE),
        ),
        in_specs=[SMEM] * 2 + [ANY] * 7,
        out_specs=[VMEM] * 4,
        scratch_shapes=[
            pltpu.VMEM((2, WIDTH, WIDTH), jnp.float32),
            pltpu.VMEM((SIDE, SIDE), jnp.float32),
            pltpu.VMEM((SIDE, SIDE), jnp.float32),
            pltpu.VMEM((COUNT, 2 * ROWS, SIDE), jnp.float32),
            TABLE_VMEM,
            pltpu.SemaphoreType.DMA((7,)),
        ],
        compiler_params=PARAMS,
        name="forward",
    )(*operands)


def inverse(*operands):
    return pl.pallas_call(
        inverse_kernel,
        out_shape=floats(PLANE_SIZE, 2, 2, 8, WIDTH),
        in_specs=[SMEM] * 2 + [VMEM] + [ANY] * 3,
        out_specs=VMEM,
        scratch_shapes=[
            pltpu.VMEM((2, WIDTH, WIDTH), jnp.float32),
            pltpu.VMEM((COUNT, 2, 2 * SIDE, SIDE), jnp.float32),
            pltpu.VMEM((2, 2, SIDE, SIDE), jnp.float32),
            TABLE_VMEM,
            pltpu.SemaphoreType.DMA((3,)),
        ],
        compiler_params=PARAMS,
        name="inverse",
    )(*operands)


def body(object_field, probe_modes, amplitude, positions):
    table = jnp.asarray(tables())
    zlo, core = lax.axis_index("zlo"), lax.axis_index("core")
    y, zhi, x = (lax.axis_index(name) for name in ("y", "zhi", "x"))
    lower_half = jnp.where((zlo == 15) & (core == 1), 1 - zhi, zhi)
    flags = jnp.stack([core, zhi, y * 4 + x, lower_half]).astype(jnp.int32)

    halo = moved(object_field, along_ring(-1))
    piece = lax.dynamic_slice(probe_modes[0], (core, zlo * ROWS, 0), (1, ROWS, SIDE))[0]
    gathered = lax.all_gather(piece, ("zhi", "zlo"), axis=0, tiled=True).reshape(2, SIDE, SIDE)
    swapped = moved(lax.dynamic_index_in_dim(gathered, 1 - zhi, 0, keepdims=False), other_core)

    far, intensity, measured, probes = forward(
        positions, flags, object_field, halo, probe_modes[0], gathered, swapped, amplitude, table
    )
    summed = jnp.sum(lax.all_to_all(intensity, PLANE, 0, 0), 0)
    change = measured / jnp.sqrt(summed + 0.05 * MODES) - 1.0
    change = lax.all_to_all(jnp.broadcast_to(change[None], intensity.shape), PLANE, 0, 0)

    gradient = inverse(positions, flags, change, far, probes, table)
    gradient = jnp.sum(lax.all_to_all(gradient, PLANE, 0, 0), 0)
    total = gradient[0] + moved(gradient[1], along_ring(1))
    own = lax.dynamic_slice_in_dim(object_field, ((y * 2 + zhi) * 4 + x) * 8, 8, 1)
    return own + 0.5 * total / MODES


def solution(mesh):
    fine = Mesh(mesh.devices.reshape(SIZES), AXES)
    tile, spec = ("zlo", "core"), ("y", "zhi", "x")
    placed = (
        P(None, tile, None),
        P(spec, None, None, None),
        P(tile, None, None),
        P(tile, None),
    )
    return jax.shard_map(
        body, mesh=fine, in_specs=placed, out_specs=P(None, tile + spec, None), check_vma=False
    )
```

```python
import math

import jax
import jax.numpy as jnp
import ml_dtypes
import numpy as np
from jax import lax
from jax.experimental import pallas as pl
from jax.experimental.pallas import tpu as pltpu
from jax.sharding import Mesh, PartitionSpec as P

AXES = ("zlo", "core", "y", "zhi", "x")
SIZES = (16, 2, 4, 2, 4)
PLANE = ("y", "x")
SIDE = 256
HALF = SIDE // 2
WIDTH = 512
COUNT = 4
MODES = 32
PLANE_SIZE = 16
ROWS = SIDE // PLANE_SIZE
SPAN = SIDE + 8


def pairs_of(move):
    count = math.prod(SIZES)
    pairs = []
    for source in range(count):
        place = np.unravel_index(source, SIZES)
        target = np.ravel_multi_index(move(*(int(v) for v in place)), SIZES)
        pairs.append((source, int(target)))
    return pairs


def along_ring(steps):
    def move(zlo, core, y, zhi, x):
        chip, core = divmod(((zhi * 16 + zlo) * 2 + core + steps) % 64, 2)
        return chip % 16, core, y, chip // 16, x

    return move


def other_core(zlo, core, y, zhi, x):
    return zlo, 1 - core, y, zhi, x


def other_half(zlo, core, y, zhi, x):
    return zlo, core, y, 1 - zhi, x


def next_chip(zlo, core, y, zhi, x):
    return zlo ^ 1, core, y, zhi, x


def next_other(zlo, core, y, zhi, x):
    return zlo ^ 1, 1 - core, y, zhi, x


def across(zlo, core, y, zhi, x):
    chip = zhi * 16 + zlo
    chip = (chip + (8 if chip // 8 % 2 else -8)) % 32
    return chip % 16, core, y, chip // 16, x


def moved(value, move):
    return lax.ppermute(value, AXES, pairs_of(move))


def tables():
    out = np.zeros((2, 2, 2, SIDE, SIDE), ml_dtypes.bfloat16)
    for parity in range(2):
        freq = 2 * np.arange(HALF) + parity
        angle = (np.outer(freq, np.arange(HALF)) % SIDE) * (2.0 * math.pi / SIDE)
        cos, sin = np.cos(angle) / 16.0, np.sin(angle) / 16.0
        whole = np.block([[cos, sin], [-sin, cos]])
        for turned, table in enumerate((whole, whole.T)):
            high = table.astype(np.float32).astype(ml_dtypes.bfloat16)
            low = (table - high.astype(np.float64)).astype(np.float32)
            out[turned, parity, 0] = high
            out[turned, parity, 1] = low.astype(ml_dtypes.bfloat16)
    return out


def halves(value):
    high = value.astype(jnp.bfloat16)
    return high, (value - high.astype(jnp.float32)).astype(jnp.bfloat16)


def dot(a, b):
    return jnp.dot(a, b, preferred_element_type=jnp.float32)


def product(a, b):
    return dot(a[0], b[0]) + (dot(a[0], b[1]) + dot(a[1], b[0]))


def side_by_side(*parts):
    return jnp.concatenate(parts, 1)


def stacked(*parts):
    return jnp.concatenate(parts, 0)


def own_share(amp, plane):
    out_row = lax.broadcasted_iota(jnp.int32, (COUNT * ROWS, COUNT * 2 * ROWS), 0)
    in_row = lax.broadcasted_iota(jnp.int32, (COUNT * ROWS, COUNT * 2 * ROWS), 1)
    take_rows = jnp.where(in_row == 2 * out_row + plane // 8, 1.0, 0.0).astype(jnp.bfloat16)
    in_col = lax.broadcasted_iota(jnp.int32, (SIDE, SIDE), 0)
    out_col = lax.broadcasted_iota(jnp.int32, (SIDE, SIDE), 1)
    wanted = jnp.where(out_col < HALF, 2 * out_col, 2 * out_col - (SIDE - 1))
    take_cols = jnp.where(in_col == wanted, 1.0, 0.0).astype(jnp.bfloat16)
    value, total = amp.reshape(COUNT * 2 * ROWS, SIDE), 0.0
    for _ in range(3):
        part = value.astype(jnp.bfloat16)
        value = value - part.astype(jnp.float32)
        total = total + dot(dot(take_rows, part).astype(jnp.bfloat16), take_cols)
    return total.reshape(COUNT, ROWS, SIDE)


def to_frequencies(waves, table):
    parts = []
    for parity, sign in ((0, 1.0), (1, -1.0)):
        blocks = [stacked(*(part[:HALF] + sign * part[HALF:] for part in wave)) for wave in waves]
        parts.append(product(times(table, 0, parity), halves(side_by_side(*blocks))))
    outs = []
    for parity, sign in ((0, 1.0), (1, -1.0)):
        blocks = []
        for w in range(2):
            middle = w * SIDE + HALF
            for part in parts:
                block = part[:, middle - HALF : middle] + sign * part[:, middle : middle + HALF]
                blocks.append(side_by_side(block[:HALF], block[HALF:]))
        outs.append(product(halves(stacked(*blocks)), times(table, 1, parity)))
    return outs


def to_samples(far, table):
    parts = []
    for parity in range(2):
        blocks = []
        for w in range(2):
            start = w * SIDE + parity * HALF
            for side in far:
                block = side[start : start + HALF]
                blocks.append(stacked(block[:, :HALF], block[:, HALF:]))
        parts.append(product(times(table, 1, parity), halves(side_by_side(*blocks))))
    both = parts[0] + parts[1], parts[0] - parts[1]
    parts = []
    for parity in range(2):
        blocks = []
        for w in range(2):
            start = (2 * w + parity) * HALF
            for rows in both:
                block = rows[:, start : start + HALF]
                blocks.append(side_by_side(block[:HALF], block[HALF:]))
        parts.append(product(halves(stacked(*blocks)), times(table, 0, parity)))
    near, away = parts[0] + parts[1], parts[0] - parts[1]
    waves = []
    for w in range(2):
        rows = slice(w * SIDE, (w + 1) * SIDE)
        waves.append(
            (
                side_by_side(near[rows, :HALF], away[rows, :HALF]),
                side_by_side(near[rows, HALF:], away[rows, HALF:]),
            )
        )
    return waves


def times(table, turned, parity):
    return table[turned, parity, 0], table[turned, parity, 1]


def lit(probe_re, probe_im, patch_re, patch_im):
    return probe_re * patch_re - probe_im * patch_im, probe_re * patch_im + probe_im * patch_re


def started(pairs, sems):
    copies = [pltpu.make_async_copy(*pair, sems.at[i]) for i, pair in enumerate(pairs)]
    for copy in copies:
        copy.start()
    return copies


def own_kernel(
    pos, halo, own_hbm, probe_hbm, table_hbm,
    far_hbm, patch_hbm, intensity, ext, probe, table, far, patch, sems, out_sems,
):
    pairs = (
        (own_hbm, ext.at[:, pl.ds(0, SIDE)]),
        (probe_hbm, probe),
        (table_hbm, table),
    )
    copies = started(pairs, sems)
    ext[:, SIDE:] = halo[...]
    for copy in copies:
        copy.wait()

    def out_copies(q):
        return (
            pltpu.make_async_copy(far.at[q], far_hbm.at[q], out_sems.at[0, q]),
            pltpu.make_async_copy(patch.at[q], patch_hbm.at[q], out_sems.at[1, q]),
        )

    def pair(q, carry):
        waves = []
        for w in range(2):
            row, col = pos[2 * q + w, 0], pos[2 * q + w, 1]
            base = pl.multiple_of(row // 8 * 8, 8)
            left = lax.rem(WIDTH - col, WIDTH)
            up = lax.rem(SPAN - (row - base), SPAN)
            window = []
            for part in range(2):
                rows = pltpu.roll(ext[part, pl.ds(base, SPAN), :], left, 1)[:, :SIDE]
                window.append(pltpu.roll(rows, up, 0)[:SIDE])
                patch[q, w, part] = window[part]
            waves.append(lit(probe[0], probe[1], *window))
        for parity, out in enumerate(to_frequencies(waves, table)):
            far[q, parity] = out
            strength = out[:, :HALF] * out[:, :HALF] + out[:, HALF:] * out[:, HALF:]
            columns = pl.ds(parity * HALF, HALF)
            for w in range(2):
                rows = strength[w * SIDE : (w + 1) * SIDE]
                intensity[:, 2 * q + w, :, columns] = rows.reshape(PLANE_SIZE, ROWS, HALF)
        for copy in out_copies(q):
            copy.start()
        return carry

    lax.fori_loop(0, COUNT // 2, pair, 0)
    for q in range(COUNT // 2):
        for copy in out_copies(q):
            copy.wait()


def other_kernel(
    flags, patch_hbm, amp_hbm, table_hbm, first, second, crossed_first, crossed_second,
    far_hbm, probe_hbm, measured, patch, amp, table, probe, far, sems, out_sems,
):
    core, plane, odd = flags[0], flags[2], flags[4]
    start = pl.multiple_of(lax.rem(plane, 8) * 2 * ROWS, 2 * ROWS)
    pairs = (
        (amp_hbm.at[:, pl.ds(start, 2 * ROWS)], amp),
        (table_hbm, table),
        (patch_hbm, patch),
    )
    copies = started(pairs, sems)
    copies[0].wait()
    measured[...] = own_share(amp[...], plane)
    for copy in copies[1:]:
        copy.wait()
    for channel in range(2):
        for half in range(2):
            of_own = jnp.where(odd == half, first[...], second[...])
            of_other = jnp.where(odd == half, crossed_first[...], crossed_second[...])
            value = jnp.where(core == channel, of_own, of_other)
            probe[channel, half * HALF : (half + 1) * HALF] = value
    probe_copy = pltpu.make_async_copy(probe, probe_hbm, out_sems.at[COUNT // 2])
    probe_copy.start()

    def far_copy(q):
        return pltpu.make_async_copy(far.at[q], far_hbm.at[q], out_sems.at[q])

    def pair(q, carry):
        waves = [lit(probe[0], probe[1], patch[q, w, 0], patch[q, w, 1]) for w in range(2)]
        for parity, out in enumerate(to_frequencies(waves, table)):
            far[q, parity] = out
        far_copy(q).start()
        return carry

    lax.fori_loop(0, COUNT // 2, pair, 0)
    for q in range(COUNT // 2):
        far_copy(q).wait()
    probe_copy.wait()


def collect_kernel(shares, piece_in, summed, piece_out):
    summed[...] = jnp.sum(shares[...], 0)
    piece_out[...] = piece_in[...]


def change_kernel(summed, arrived, measured, out):
    total = summed[...] + arrived[...]
    change = measured[...] / jnp.sqrt(total + 0.05 * MODES) - 1.0
    for d in range(PLANE_SIZE):
        out[d] = change


def inverse_kernel(
    pos, flags, change, far_own_hbm, far_other_hbm, probe_own_hbm, probe_other_hbm, table_hbm,
    out, grad, far, probe, table, sems, far_sems,
):
    pairs = ((probe_own_hbm, probe.at[0]), (probe_other_hbm, probe.at[1]), (table_hbm, table))
    copies = started(pairs, sems)

    def far_copies(q):
        return [
            pltpu.make_async_copy(source.at[q], far.at[m, q], far_sems.at[m, q])
            for m, source in enumerate((far_own_hbm, far_other_hbm))
        ]

    for q in range(COUNT // 2):
        for copy in far_copies(q):
            copy.start()
    grad[...] = jnp.zeros_like(grad)
    for copy in copies:
        copy.wait()

    def pair(q, carry):
        for copy in far_copies(q):
            copy.wait()
        factors = []
        for parity in range(2):
            columns = pl.ds(parity * HALF, HALF)
            rows = [change[:, 2 * q + w, :, columns].reshape(SIDE, HALF) for w in range(2)]
            factors.append(side_by_side(stacked(*rows), stacked(*rows)))
        adds = [[0.0, 0.0], [0.0, 0.0]]
        for m in range(2):
            waves = to_samples([far[m, q, side] * factors[side] for side in range(2)], table)
            for add, (real, imag) in zip(adds, waves):
                add[0] += probe[m, 0] * real + probe[m, 1] * imag
                add[1] += probe[m, 0] * imag - probe[m, 1] * real
        below = jnp.zeros((SPAN - SIDE, SIDE), jnp.float32)
        beside = jnp.zeros((SPAN, WIDTH - SIDE), jnp.float32)
        for w in range(2):
            row, col = pos[2 * q + w, 0], pos[2 * q + w, 1]
            base = pl.multiple_of(row // 8 * 8, 8)
            for part in range(2):
                placed = pltpu.roll(stacked(adds[w][part], below), row - base, 0)
                placed = pltpu.roll(side_by_side(placed, beside), col, 1)
                grad[part, pl.ds(base, SPAN), :] += placed
        return carry

    lax.fori_loop(0, COUNT // 2, pair, 0)
    for d in range(PLANE_SIZE):
        for lower in range(2):
            start = lower * SIDE + (d // 4) * 64 + flags[1 + 2 * lower] * 32 + (d % 4) * 8
            out[d, lower] = grad[:, pl.ds(pl.multiple_of(start, 8), 8), :]


VMEM = pl.BlockSpec(memory_space=pltpu.VMEM)
SMEM = pl.BlockSpec(memory_space=pltpu.SMEM)
HBM = pl.BlockSpec(memory_space=pltpu.HBM)
PAIRS = COUNT // 2
FAR = (PAIRS, 2, 2 * SIDE, SIDE)
PATCH = (PAIRS, 2, 2, SIDE, SIDE)
DMA = pltpu.SemaphoreType.DMA


def floats(*shape):
    return jax.ShapeDtypeStruct(shape, jnp.float32)


def scratch(*shape):
    return pltpu.VMEM(shape, jnp.float32)


TABLE = pltpu.VMEM((2, 2, 2, SIDE, SIDE), jnp.bfloat16)


def call(kernel, name, in_specs, outs, scratches, operands, work=0, limit=32):
    moves = sum(math.prod(v.shape) * v.dtype.itemsize for v in operands)
    return pl.pallas_call(
        kernel,
        out_shape=[shape for shape, _ in outs],
        in_specs=in_specs,
        out_specs=[spec for _, spec in outs],
        scratch_shapes=scratches,
        compiler_params=pltpu.CompilerParams(vmem_limit_bytes=limit * 1024 * 1024),
        cost_estimate=pl.CostEstimate(flops=work, bytes_accessed=moves, transcendentals=0),
        name=name,
    )(*operands)


def body(object_field, probe_modes, amplitude, positions):
    table = jnp.asarray(tables())
    work = COUNT * 12 * 2 * SIDE**3
    zlo, core = lax.axis_index("zlo"), lax.axis_index("core")
    y, zhi, x = (lax.axis_index(name) for name in ("y", "zhi", "x"))
    odd = lax.rem(zlo, 2)
    lower_half = jnp.where((zlo == 15) & (core == 1), 1 - zhi, zhi)
    flags = jnp.stack([core, zhi, y * 4 + x, lower_half, odd]).astype(jnp.int32)
    probe = probe_modes[0]

    halo = moved(object_field, along_ring(-1))
    piece = lax.dynamic_slice(probe, (core, odd * HALF, 0), (1, HALF, SIDE))[0]
    first = moved(piece, across)
    far_own, patches, intensity = call(
        own_kernel,
        "own",
        [SMEM, VMEM] + [HBM] * 3,
        [(floats(*FAR), HBM), (floats(*PATCH), HBM), (floats(PLANE_SIZE, COUNT, ROWS, SIDE), VMEM)],
        [
            scratch(2, WIDTH, WIDTH),
            scratch(2, SIDE, SIDE),
            TABLE,
            scratch(*FAR),
            scratch(*PATCH),
            DMA((3,)),
            DMA((2, PAIRS)),
        ],
        (positions, halo, object_field, probe, table),
        work,
    )
    shares = lax.all_to_all(intensity, PLANE, 0, 0)
    summed, first = call(
        collect_kernel,
        "collect",
        [VMEM] * 2,
        [(floats(COUNT, ROWS, SIDE), VMEM), (floats(HALF, SIDE), VMEM)],
        [],
        (shares, first),
    )
    arrived = moved(summed, other_half)
    others = [moved(first, move) for move in (next_chip, other_core, next_other)]
    far_other, probe_other, measured = call(
        other_kernel,
        "other",
        [SMEM] + [HBM] * 3 + [VMEM] * 4,
        [(floats(*FAR), HBM), (floats(2, SIDE, SIDE), HBM), (floats(COUNT, ROWS, SIDE), VMEM)],
        [
            scratch(*PATCH),
            scratch(COUNT, 2 * ROWS, SIDE),
            TABLE,
            scratch(2, SIDE, SIDE),
            scratch(*FAR),
            DMA((3,)),
            DMA((PAIRS + 1,)),
        ],
        (flags, patches, amplitude, table, first, *others),
        work,
    )
    (change,) = call(
        change_kernel,
        "change",
        [VMEM] * 3,
        [(floats(PLANE_SIZE, COUNT, ROWS, SIDE), VMEM)],
        [],
        (summed, arrived, measured),
    )
    change = lax.all_to_all(change, PLANE, 0, 0)
    (gradient,) = call(
        inverse_kernel,
        "inverse",
        [SMEM] * 2 + [VMEM] + [HBM] * 5,
        [(floats(PLANE_SIZE, 2, 2, 8, WIDTH), VMEM)],
        [
            scratch(2, WIDTH, WIDTH),
            scratch(2, *FAR),
            scratch(2, 2, SIDE, SIDE),
            TABLE,
            DMA((3,)),
            DMA((2, PAIRS)),
        ],
        (positions, flags, change, far_own, far_other, probe, probe_other, table),
        2 * work,
    )
    gradient = jnp.sum(lax.all_to_all(gradient, PLANE, 0, 0), 0)
    total = gradient[0] + moved(gradient[1], along_ring(1))
    own = lax.dynamic_slice_in_dim(object_field, ((y * 2 + zhi) * 4 + x) * 8, 8, 1)
    return own + 0.5 * total / MODES


def solution(mesh):
    fine = Mesh(mesh.devices.reshape(SIZES), AXES)
    tile, spec = ("zlo", "core"), ("y", "zhi", "x")
    placed = (
        P(None, tile, None),
        P(spec, None, None, None),
        P(tile, None, None),
        P(tile, None),
    )
    return jax.shard_map(
        body, mesh=fine, in_specs=placed, out_specs=P(None, tile + spec, None), check_vma=False
    )
```

```python
import math

import jax
import jax.numpy as jnp
import ml_dtypes
import numpy as np
from jax import lax
from jax.experimental import pallas as pl
from jax.experimental.pallas import tpu as pltpu
from jax.sharding import Mesh, PartitionSpec as P

AXES = ("zlo", "core", "y", "zhi", "x")
SIZES = (16, 2, 4, 2, 4)
PLANE = ("y", "x")
SIDE = 256
HALF = SIDE // 2
QUARTER = SIDE // 4
WIDTH = 512
COUNT = 4
MODES = 32
PLANE_SIZE = 16
ROWS = SIDE // PLANE_SIZE
SPAN = SIDE + 8


def pairs_of(move):
    count = math.prod(SIZES)
    pairs = []
    for source in range(count):
        place = np.unravel_index(source, SIZES)
        target = np.ravel_multi_index(move(*(int(v) for v in place)), SIZES)
        pairs.append((source, int(target)))
    return pairs


def along_ring(steps):
    def move(zlo, core, y, zhi, x):
        chip, core = divmod(((zhi * 16 + zlo) * 2 + core + steps) % 64, 2)
        return chip % 16, core, y, chip // 16, x

    return move


def other_core(zlo, core, y, zhi, x):
    return zlo, 1 - core, y, zhi, x


def other_half(zlo, core, y, zhi, x):
    return zlo, core, y, 1 - zhi, x


def next_chip(zlo, core, y, zhi, x):
    return zlo ^ 1, core, y, zhi, x


def two_on(zlo, core, y, zhi, x):
    return zlo ^ 2, core, y, zhi, x


def two_on_other(zlo, core, y, zhi, x):
    return zlo ^ 2, 1 - core, y, zhi, x


def across(zlo, core, y, zhi, x):
    chip = zhi * 16 + zlo
    chip = (chip + (8 if chip // 8 % 2 else -8)) % 32
    return chip % 16, core, y, chip // 16, x


def moved(value, move):
    return lax.ppermute(value, AXES, pairs_of(move))


def tables():
    out = np.zeros((2, 2, 2, SIDE, SIDE), ml_dtypes.bfloat16)
    for parity in range(2):
        freq = 2 * np.arange(HALF) + parity
        angle = (np.outer(freq, np.arange(HALF)) % SIDE) * (2.0 * math.pi / SIDE)
        cos, sin = np.cos(angle) / 16.0, np.sin(angle) / 16.0
        whole = np.block([[cos, sin], [-sin, cos]])
        for turned, table in enumerate((whole, whole.T)):
            high = table.astype(np.float32).astype(ml_dtypes.bfloat16)
            low = (table - high.astype(np.float64)).astype(np.float32)
            out[turned, parity, 0] = high
            out[turned, parity, 1] = low.astype(ml_dtypes.bfloat16)
    return out


def halves(value):
    high = value.astype(jnp.bfloat16)
    return high, (value - high.astype(jnp.float32)).astype(jnp.bfloat16)


def dot(a, b):
    return jnp.dot(a, b, preferred_element_type=jnp.float32)


def product(a, b):
    return dot(a[0], b[0]) + (dot(a[0], b[1]) + dot(a[1], b[0]))


def side_by_side(*parts):
    return jnp.concatenate(parts, 1)


def stacked(*parts):
    return jnp.concatenate(parts, 0)


def own_share(amp, plane):
    out_row = lax.broadcasted_iota(jnp.int32, (COUNT * ROWS, COUNT * 2 * ROWS), 0)
    in_row = lax.broadcasted_iota(jnp.int32, (COUNT * ROWS, COUNT * 2 * ROWS), 1)
    take_rows = jnp.where(in_row == 2 * out_row + plane // 8, 1.0, 0.0).astype(jnp.bfloat16)
    in_col = lax.broadcasted_iota(jnp.int32, (SIDE, SIDE), 0)
    out_col = lax.broadcasted_iota(jnp.int32, (SIDE, SIDE), 1)
    wanted = jnp.where(out_col < HALF, 2 * out_col, 2 * out_col - (SIDE - 1))
    take_cols = jnp.where(in_col == wanted, 1.0, 0.0).astype(jnp.bfloat16)
    value, total = amp.reshape(COUNT * 2 * ROWS, SIDE), 0.0
    for _ in range(3):
        part = value.astype(jnp.bfloat16)
        value = value - part.astype(jnp.float32)
        total = total + dot(dot(take_rows, part).astype(jnp.bfloat16), take_cols)
    return total.reshape(COUNT, ROWS, SIDE)


def to_frequencies(waves, table):
    parts = []
    for parity, sign in ((0, 1.0), (1, -1.0)):
        blocks = [stacked(*(part[:HALF] + sign * part[HALF:] for part in wave)) for wave in waves]
        parts.append(product(times(table, 0, parity), halves(side_by_side(*blocks))))
    outs = []
    for parity, sign in ((0, 1.0), (1, -1.0)):
        blocks = []
        for w in range(2):
            middle = w * SIDE + HALF
            for part in parts:
                block = part[:, middle - HALF : middle] + sign * part[:, middle : middle + HALF]
                blocks.append(side_by_side(block[:HALF], block[HALF:]))
        outs.append(product(halves(stacked(*blocks)), times(table, 1, parity)))
    return outs


def to_samples(far, table):
    parts = []
    for parity in range(2):
        blocks = []
        for w in range(2):
            start = w * SIDE + parity * HALF
            for side in far:
                block = side[start : start + HALF]
                blocks.append(stacked(block[:, :HALF], block[:, HALF:]))
        parts.append(product(times(table, 1, parity), halves(side_by_side(*blocks))))
    both = parts[0] + parts[1], parts[0] - parts[1]
    parts = []
    for parity in range(2):
        blocks = []
        for w in range(2):
            start = (2 * w + parity) * HALF
            for rows in both:
                block = rows[:, start : start + HALF]
                blocks.append(side_by_side(block[:HALF], block[HALF:]))
        parts.append(product(halves(stacked(*blocks)), times(table, 0, parity)))
    near, away = parts[0] + parts[1], parts[0] - parts[1]
    waves = []
    for w in range(2):
        rows = slice(w * SIDE, (w + 1) * SIDE)
        waves.append(
            (
                side_by_side(near[rows, :HALF], away[rows, :HALF]),
                side_by_side(near[rows, HALF:], away[rows, HALF:]),
            )
        )
    return waves


def times(table, turned, parity):
    return table[turned, parity, 0], table[turned, parity, 1]


def lit(probe_re, probe_im, patch_re, patch_im):
    return probe_re * patch_re - probe_im * patch_im, probe_re * patch_im + probe_im * patch_re


def started(pairs, sems):
    copies = [pltpu.make_async_copy(*pair, sems.at[i]) for i, pair in enumerate(pairs)]
    for copy in copies:
        copy.start()
    return copies


def own_kernel(
    pos, halo, own_hbm, probe_hbm, table_hbm, _,
    far_hbm, patch_hbm, intensity, ext, probe, table, far, patch, sems, out_sems,
):
    pairs = (
        (own_hbm, ext.at[:, pl.ds(0, SIDE)]),
        (probe_hbm, probe),
        (table_hbm, table),
    )
    copies = started(pairs, sems)
    ext[:, SIDE:] = halo[...]
    for copy in copies:
        copy.wait()

    def out_copies(q):
        return (
            pltpu.make_async_copy(far.at[q], far_hbm.at[q], out_sems.at[0, q]),
            pltpu.make_async_copy(patch.at[q], patch_hbm.at[q], out_sems.at[1, q]),
        )

    def pair(q, carry):
        waves = []
        for w in range(2):
            row, col = pos[2 * q + w, 0], pos[2 * q + w, 1]
            base = pl.multiple_of(row // 8 * 8, 8)
            left = lax.rem(WIDTH - col, WIDTH)
            up = lax.rem(SPAN - (row - base), SPAN)
            window = []
            for part in range(2):
                rows = pltpu.roll(ext[part, pl.ds(base, SPAN), :], left, 1)[:, :SIDE]
                window.append(pltpu.roll(rows, up, 0)[:SIDE])
                patch[q, w, part] = window[part]
            waves.append(lit(probe[0], probe[1], *window))
        for parity, out in enumerate(to_frequencies(waves, table)):
            far[q, parity] = out
            strength = out[:, :HALF] * out[:, :HALF] + out[:, HALF:] * out[:, HALF:]
            columns = pl.ds(parity * HALF, HALF)
            for w in range(2):
                rows = strength[w * SIDE : (w + 1) * SIDE]
                intensity[:, 2 * q + w, :, columns] = rows.reshape(PLANE_SIZE, ROWS, HALF)
        for copy in out_copies(q):
            copy.start()
        return carry

    lax.fori_loop(0, COUNT // 2, pair, 0)
    for q in range(COUNT // 2):
        for copy in out_copies(q):
            copy.wait()


def other_kernel(
    flags, patch_hbm, amp_hbm, table_hbm, block, next_block,
    far_hbm, probe_hbm, measured, patch, amp, table, probe, far, sems, out_sems,
):
    core, plane, quarter = flags[0], flags[2], flags[4]
    start = pl.multiple_of(lax.rem(plane, 8) * 2 * ROWS, 2 * ROWS)
    pairs = (
        (amp_hbm.at[:, pl.ds(start, 2 * ROWS)], amp),
        (table_hbm, table),
        (patch_hbm, patch),
    )
    copies = started(pairs, sems)
    copies[0].wait()
    measured[...] = own_share(amp[...], plane)
    for copy in copies[1:]:
        copy.wait()
    for channel in range(2):
        for part in range(SIDE // QUARTER):
            apart = jnp.bitwise_xor(quarter, part)
            place = jnp.bitwise_xor(core, channel), apart // 2
            value = jnp.where(apart % 2 == 0, block[place], next_block[place])
            probe[channel, part * QUARTER : (part + 1) * QUARTER] = value
    probe_copy = pltpu.make_async_copy(probe, probe_hbm, out_sems.at[COUNT // 2])
    probe_copy.start()

    def far_copy(q):
        return pltpu.make_async_copy(far.at[q], far_hbm.at[q], out_sems.at[q])

    def pair(q, carry):
        waves = [lit(probe[0], probe[1], patch[q, w, 0], patch[q, w, 1]) for w in range(2)]
        for parity, out in enumerate(to_frequencies(waves, table)):
            far[q, parity] = out
        far_copy(q).start()
        return carry

    lax.fori_loop(0, COUNT // 2, pair, 0)
    for q in range(COUNT // 2):
        far_copy(q).wait()
    probe_copy.wait()


def collect_kernel(shares, first, second, crossed_first, crossed_second, summed, block):
    summed[...] = jnp.sum(shares[...], 0)
    block[0, 0] = first[...]
    block[0, 1] = second[...]
    block[1, 0] = crossed_first[...]
    block[1, 1] = crossed_second[...]


def change_kernel(summed, arrived, measured, out):
    total = summed[...] + arrived[...]
    change = measured[...] / jnp.sqrt(total + 0.05 * MODES) - 1.0
    for d in range(PLANE_SIZE):
        out[d] = change


def inverse_kernel(
    pos, flags, change, far_own_hbm, far_other_hbm, probe_own_hbm, probe_other_hbm, table_hbm,
    out, grad, far, probe, table, sems, far_sems,
):
    pairs = ((probe_own_hbm, probe.at[0]), (probe_other_hbm, probe.at[1]), (table_hbm, table))
    copies = started(pairs, sems)

    def far_copies(q):
        return [
            pltpu.make_async_copy(source.at[q], far.at[m, q], far_sems.at[m, q])
            for m, source in enumerate((far_own_hbm, far_other_hbm))
        ]

    for q in range(COUNT // 2):
        for copy in far_copies(q):
            copy.start()
    grad[...] = jnp.zeros_like(grad)
    for copy in copies:
        copy.wait()

    def pair(q, carry):
        for copy in far_copies(q):
            copy.wait()
        factors = []
        for parity in range(2):
            columns = pl.ds(parity * HALF, HALF)
            rows = [change[:, 2 * q + w, :, columns].reshape(SIDE, HALF) for w in range(2)]
            factors.append(side_by_side(stacked(*rows), stacked(*rows)))
        adds = [[0.0, 0.0], [0.0, 0.0]]
        for m in range(2):
            waves = to_samples([far[m, q, side] * factors[side] for side in range(2)], table)
            for add, (real, imag) in zip(adds, waves):
                add[0] += probe[m, 0] * real + probe[m, 1] * imag
                add[1] += probe[m, 0] * imag - probe[m, 1] * real
        below = jnp.zeros((SPAN - SIDE, SIDE), jnp.float32)
        beside = jnp.zeros((SPAN, WIDTH - SIDE), jnp.float32)
        for w in range(2):
            row, col = pos[2 * q + w, 0], pos[2 * q + w, 1]
            base = pl.multiple_of(row // 8 * 8, 8)
            for part in range(2):
                placed = pltpu.roll(stacked(adds[w][part], below), row - base, 0)
                placed = pltpu.roll(side_by_side(placed, beside), col, 1)
                grad[part, pl.ds(base, SPAN), :] += placed
        return carry

    lax.fori_loop(0, COUNT // 2, pair, 0)
    for d in range(PLANE_SIZE):
        for lower in range(2):
            start = lower * SIDE + (d // 4) * 64 + flags[1 + 2 * lower] * 32 + (d % 4) * 8
            out[d, lower] = grad[:, pl.ds(pl.multiple_of(start, 8), 8), :]


VMEM = pl.BlockSpec(memory_space=pltpu.VMEM)
SMEM = pl.BlockSpec(memory_space=pltpu.SMEM)
HBM = pl.BlockSpec(memory_space=pltpu.HBM)
PAIRS = COUNT // 2
LIMIT = 60
FAR = (PAIRS, 2, 2 * SIDE, SIDE)
PATCH = (PAIRS, 2, 2, SIDE, SIDE)
DMA = pltpu.SemaphoreType.DMA


def floats(*shape):
    return jax.ShapeDtypeStruct(shape, jnp.float32)


def scratch(*shape):
    return pltpu.VMEM(shape, jnp.float32)


TABLE = pltpu.VMEM((2, 2, 2, SIDE, SIDE), jnp.bfloat16)


def call(kernel, name, in_specs, outs, scratches, operands, work=0, limit=LIMIT):
    moves = sum(math.prod(v.shape) * v.dtype.itemsize for v in operands)
    return pl.pallas_call(
        kernel,
        out_shape=[shape for shape, _ in outs],
        in_specs=in_specs,
        out_specs=[spec for _, spec in outs],
        scratch_shapes=scratches,
        compiler_params=pltpu.CompilerParams(vmem_limit_bytes=limit * 1024 * 1024),
        cost_estimate=pl.CostEstimate(flops=work, bytes_accessed=moves, transcendentals=0),
        name=name,
    )(*operands)


def body(object_field, probe_modes, amplitude, positions):
    table = jnp.asarray(tables())
    work = COUNT * 12 * 2 * SIDE**3
    zlo, core = lax.axis_index("zlo"), lax.axis_index("core")
    y, zhi, x = (lax.axis_index(name) for name in ("y", "zhi", "x"))
    quarter = lax.rem(zlo, 4)
    lower_half = jnp.where((zlo == 15) & (core == 1), 1 - zhi, zhi)
    flags = jnp.stack([core, zhi, y * 4 + x, lower_half, quarter]).astype(jnp.int32)
    probe = probe_modes[0]

    halo = moved(object_field, along_ring(-1))
    piece = lax.dynamic_slice(probe, (core, quarter * QUARTER, 0), (1, QUARTER, SIDE))[0]
    first = moved(piece, across)
    far_own, patches, intensity = call(
        own_kernel,
        "own",
        [SMEM, VMEM] + [HBM] * 4,
        [(floats(*FAR), HBM), (floats(*PATCH), HBM), (floats(PLANE_SIZE, COUNT, ROWS, SIDE), VMEM)],
        [
            scratch(2, WIDTH, WIDTH),
            scratch(2, SIDE, SIDE),
            TABLE,
            scratch(*FAR),
            scratch(*PATCH),
            DMA((3,)),
            DMA((2, PAIRS)),
        ],
        (positions, halo, object_field, probe, table, first),
        work,
    )
    shares = lax.all_to_all(intensity, PLANE, 0, 0)
    spread = [moved(first, move) for move in (two_on, other_core, two_on_other)]
    summed, block = call(
        collect_kernel,
        "collect",
        [VMEM] * 5,
        [(floats(COUNT, ROWS, SIDE), VMEM), (floats(2, 2, QUARTER, SIDE), VMEM)],
        [],
        (shares, first, *spread),
        limit=32,
    )
    arrived = moved(summed, other_half)
    next_block = moved(block, next_chip)
    far_other, probe_other, measured = call(
        other_kernel,
        "other",
        [SMEM] + [HBM] * 3 + [VMEM] * 2,
        [(floats(*FAR), HBM), (floats(2, SIDE, SIDE), HBM), (floats(COUNT, ROWS, SIDE), VMEM)],
        [
            scratch(*PATCH),
            scratch(COUNT, 2 * ROWS, SIDE),
            TABLE,
            scratch(2, SIDE, SIDE),
            scratch(*FAR),
            DMA((3,)),
            DMA((PAIRS + 1,)),
        ],
        (flags, patches, amplitude, table, block, next_block),
        work,
    )
    (change,) = call(
        change_kernel,
        "change",
        [VMEM] * 3,
        [(floats(PLANE_SIZE, COUNT, ROWS, SIDE), VMEM)],
        [],
        (summed, arrived, measured),
        limit=32,
    )
    change = lax.all_to_all(change, PLANE, 0, 0)
    (gradient,) = call(
        inverse_kernel,
        "inverse",
        [SMEM] * 2 + [VMEM] + [HBM] * 5,
        [(floats(PLANE_SIZE, 2, 2, 8, WIDTH), VMEM)],
        [
            scratch(2, WIDTH, WIDTH),
            scratch(2, *FAR),
            scratch(2, 2, SIDE, SIDE),
            TABLE,
            DMA((3,)),
            DMA((2, PAIRS)),
        ],
        (positions, flags, change, far_own, far_other, probe, probe_other, table),
        2 * work,
    )
    gradient = jnp.sum(lax.all_to_all(gradient, PLANE, 0, 0), 0)
    total = gradient[0] + moved(gradient[1], along_ring(1))
    own = lax.dynamic_slice_in_dim(object_field, ((y * 2 + zhi) * 4 + x) * 8, 8, 1)
    return own + 0.5 * total / MODES


def solution(mesh):
    fine = Mesh(mesh.devices.reshape(SIZES), AXES)
    tile, spec = ("zlo", "core"), ("y", "zhi", "x")
    placed = (
        P(None, tile, None),
        P(spec, None, None, None),
        P(tile, None, None),
        P(tile, None),
    )
    return jax.shard_map(
        body, mesh=fine, in_specs=placed, out_specs=P(None, tile + spec, None), check_vma=False
    )
```

```python
import math

import jax
import jax.numpy as jnp
import ml_dtypes
import numpy as np
from jax import lax
from jax.experimental import pallas as pl
from jax.experimental.pallas import tpu as pltpu
from jax.sharding import Mesh, PartitionSpec as P

AXES = ("zlo", "core", "y", "zhi", "x")
SIZES = (16, 2, 4, 2, 4)
PLANE = ("y", "x")
SIDE = 256
HALF = SIDE // 2
QUARTER = SIDE // 4
WIDTH = 512
COUNT = 4
MODES = 32
PLANE_SIZE = 16
ROWS = SIDE // PLANE_SIZE
SPAN = SIDE + 8


def pairs_of(move):
    count = math.prod(SIZES)
    pairs = []
    for source in range(count):
        place = np.unravel_index(source, SIZES)
        target = np.ravel_multi_index(move(*(int(v) for v in place)), SIZES)
        pairs.append((source, int(target)))
    return pairs


def along_ring(steps):
    def move(zlo, core, y, zhi, x):
        chip, core = divmod(((zhi * 16 + zlo) * 2 + core + steps) % 64, 2)
        return chip % 16, core, y, chip // 16, x

    return move


def other_core(zlo, core, y, zhi, x):
    return zlo, 1 - core, y, zhi, x


def other_half(zlo, core, y, zhi, x):
    return zlo, core, y, 1 - zhi, x


def next_chip(zlo, core, y, zhi, x):
    return zlo ^ 1, core, y, zhi, x


def two_on(zlo, core, y, zhi, x):
    return zlo ^ 2, core, y, zhi, x


def two_on_other(zlo, core, y, zhi, x):
    return zlo ^ 2, 1 - core, y, zhi, x


def across(zlo, core, y, zhi, x):
    chip = zhi * 16 + zlo
    chip = (chip + (8 if chip // 8 % 2 else -8)) % 32
    return chip % 16, core, y, chip // 16, x


def moved(value, move):
    return lax.ppermute(value, AXES, pairs_of(move))


def tables():
    out = np.zeros((2, 2, 2, SIDE, SIDE), ml_dtypes.bfloat16)
    for parity in range(2):
        freq = 2 * np.arange(HALF) + parity
        angle = (np.outer(freq, np.arange(HALF)) % SIDE) * (2.0 * math.pi / SIDE)
        cos, sin = np.cos(angle) / 16.0, np.sin(angle) / 16.0
        whole = np.block([[cos, sin], [-sin, cos]])
        for turned, table in enumerate((whole, whole.T)):
            high = table.astype(np.float32).astype(ml_dtypes.bfloat16)
            low = (table - high.astype(np.float64)).astype(np.float32)
            out[turned, parity, 0] = high
            out[turned, parity, 1] = low.astype(ml_dtypes.bfloat16)
    return out


def halves(value):
    high = value.astype(jnp.bfloat16)
    return high, (value - high.astype(jnp.float32)).astype(jnp.bfloat16)


def dot(a, b):
    return jnp.dot(a, b, preferred_element_type=jnp.float32)


def product(a, b):
    return dot(a[0], b[0]) + (dot(a[0], b[1]) + dot(a[1], b[0]))


def side_by_side(*parts):
    return jnp.concatenate(parts, 1)


def stacked(*parts):
    return jnp.concatenate(parts, 0)


def own_share(amp, plane):
    out_row = lax.broadcasted_iota(jnp.int32, (COUNT * ROWS, COUNT * 2 * ROWS), 0)
    in_row = lax.broadcasted_iota(jnp.int32, (COUNT * ROWS, COUNT * 2 * ROWS), 1)
    take_rows = jnp.where(in_row == 2 * out_row + plane // 8, 1.0, 0.0).astype(jnp.bfloat16)
    in_col = lax.broadcasted_iota(jnp.int32, (SIDE, SIDE), 0)
    out_col = lax.broadcasted_iota(jnp.int32, (SIDE, SIDE), 1)
    wanted = jnp.where(out_col < HALF, 2 * out_col, 2 * out_col - (SIDE - 1))
    take_cols = jnp.where(in_col == wanted, 1.0, 0.0).astype(jnp.bfloat16)
    value, total = amp.reshape(COUNT * 2 * ROWS, SIDE), 0.0
    for _ in range(3):
        part = value.astype(jnp.bfloat16)
        value = value - part.astype(jnp.float32)
        total = total + dot(dot(take_rows, part).astype(jnp.bfloat16), take_cols)
    return total.reshape(COUNT, ROWS, SIDE)


def to_frequencies(waves, table):
    parts = []
    for parity, sign in ((0, 1.0), (1, -1.0)):
        blocks = [stacked(*(part[:HALF] + sign * part[HALF:] for part in wave)) for wave in waves]
        parts.append(product(times(table, 0, parity), halves(side_by_side(*blocks))))
    outs = []
    for parity, sign in ((0, 1.0), (1, -1.0)):
        blocks = []
        for w in range(2):
            middle = w * SIDE + HALF
            for part in parts:
                block = part[:, middle - HALF : middle] + sign * part[:, middle : middle + HALF]
                blocks.append(side_by_side(block[:HALF], block[HALF:]))
        outs.append(product(halves(stacked(*blocks)), times(table, 1, parity)))
    return outs


def to_samples(far, table):
    parts = []
    for parity in range(2):
        blocks = []
        for w in range(2):
            start = w * SIDE + parity * HALF
            for side in far:
                block = side[start : start + HALF]
                blocks.append(stacked(block[:, :HALF], block[:, HALF:]))
        parts.append(product(times(table, 1, parity), halves(side_by_side(*blocks))))
    both = parts[0] + parts[1], parts[0] - parts[1]
    parts = []
    for parity in range(2):
        blocks = []
        for w in range(2):
            start = (2 * w + parity) * HALF
            for rows in both:
                block = rows[:, start : start + HALF]
                blocks.append(side_by_side(block[:HALF], block[HALF:]))
        parts.append(product(halves(stacked(*blocks)), times(table, 0, parity)))
    near, away = parts[0] + parts[1], parts[0] - parts[1]
    waves = []
    for w in range(2):
        rows = slice(w * SIDE, (w + 1) * SIDE)
        waves.append(
            (
                side_by_side(near[rows, :HALF], away[rows, :HALF]),
                side_by_side(near[rows, HALF:], away[rows, HALF:]),
            )
        )
    return waves


def times(table, turned, parity):
    return table[turned, parity, 0], table[turned, parity, 1]


def lit(probe_re, probe_im, patch_re, patch_im):
    return probe_re * patch_re - probe_im * patch_im, probe_re * patch_im + probe_im * patch_re


def windows(pos, ext, pattern):
    row, col = pos[pattern, 0], pos[pattern, 1]
    base = pl.multiple_of(row // 8 * 8, 8)
    left = lax.rem(WIDTH - col, WIDTH)
    up = lax.rem(SPAN - (row - base), SPAN)
    out = []
    for part in range(2):
        rows = pltpu.roll(ext[part, pl.ds(base, SPAN), :], left, 1)[:, :SIDE]
        out.append(pltpu.roll(rows, up, 0)[:SIDE])
    return out


def started(pairs, sems):
    copies = [pltpu.make_async_copy(*pair, sems.at[i]) for i, pair in enumerate(pairs)]
    for copy in copies:
        copy.start()
    return copies


def own_kernel(
    pos, own_hbm, halo_hbm, probe_hbm, table_hbm,
    far_hbm, intensity_hbm, ext, probe, table, far, intensity, sems, out_sems,
):
    pairs = (
        (own_hbm, ext.at[:, pl.ds(0, SIDE)]),
        (halo_hbm, ext.at[:, pl.ds(SIDE, SIDE)]),
        (probe_hbm, probe),
        (table_hbm, table),
    )
    for copy in started(pairs, sems):
        copy.wait()

    def out_copies(q):
        rows = pl.ds(2 * q, 2)
        return (
            pltpu.make_async_copy(
                intensity.at[:, rows], intensity_hbm.at[:, rows], out_sems.at[1, q]
            ),
            pltpu.make_async_copy(far.at[q], far_hbm.at[q], out_sems.at[0, q]),
        )

    def pair(q, carry):
        waves = [lit(probe[0], probe[1], *windows(pos, ext, 2 * q + w)) for w in range(2)]
        for parity, out in enumerate(to_frequencies(waves, table)):
            far[q, parity] = out
            strength = out[:, :HALF] * out[:, :HALF] + out[:, HALF:] * out[:, HALF:]
            columns = pl.ds(parity * HALF, HALF)
            for w in range(2):
                rows = strength[w * SIDE : (w + 1) * SIDE]
                intensity[:, 2 * q + w, :, columns] = rows.reshape(PLANE_SIZE, ROWS, HALF)
        for copy in out_copies(q):
            copy.start()
        return carry

    lax.fori_loop(0, PAIRS, pair, 0)
    for q in range(PAIRS):
        for copy in out_copies(q):
            copy.wait()


def gate_kernel(array, _, out):
    pass


def other_kernel(
    pos, flags, own_hbm, halo_hbm, amp_hbm, table_hbm, block, next_block,
    far_hbm, probe_hbm, measured, ext, amp, table, probe, far, sems, out_sems,
):
    core, plane, quarter = flags[0], flags[2], flags[4]
    start = pl.multiple_of(lax.rem(plane, 8) * 2 * ROWS, 2 * ROWS)
    pairs = (
        (amp_hbm.at[:, pl.ds(start, 2 * ROWS)], amp),
        (table_hbm, table),
        (own_hbm, ext.at[:, pl.ds(0, SIDE)]),
        (halo_hbm, ext.at[:, pl.ds(SIDE, SIDE)]),
    )
    copies = started(pairs, sems)
    copies[0].wait()
    measured[...] = own_share(amp[...], plane)
    for copy in copies[1:]:
        copy.wait()
    for channel in range(2):
        for part in range(SIDE // QUARTER):
            apart = jnp.bitwise_xor(quarter, part)
            place = jnp.bitwise_xor(core, channel), apart // 2
            value = jnp.where(apart % 2 == 0, block[place], next_block[place])
            probe[channel, part * QUARTER : (part + 1) * QUARTER] = value
    probe_copy = pltpu.make_async_copy(probe, probe_hbm, out_sems.at[COUNT // 2])
    probe_copy.start()

    def far_copy(q):
        return pltpu.make_async_copy(far.at[q], far_hbm.at[q], out_sems.at[q])

    def pair(q, carry):
        waves = [lit(probe[0], probe[1], *windows(pos, ext, 2 * q + w)) for w in range(2)]
        for parity, out in enumerate(to_frequencies(waves, table)):
            far[q, parity] = out
        far_copy(q).start()
        return carry

    lax.fori_loop(0, COUNT // 2, pair, 0)
    for q in range(COUNT // 2):
        far_copy(q).wait()
    probe_copy.wait()


def collect_kernel(shares, first, second, crossed_first, crossed_second, summed, block):
    summed[...] = jnp.sum(shares[...], 0)
    block[0, 0] = first[...]
    block[0, 1] = second[...]
    block[1, 0] = crossed_first[...]
    block[1, 1] = crossed_second[...]


def change_kernel(summed, arrived, measured, out):
    total = summed[...] + arrived[...]
    change = measured[...] / jnp.sqrt(total + 0.05 * MODES) - 1.0
    for d in range(PLANE_SIZE):
        out[d] = change


def inverse_kernel(
    pos, flags, change, far_own_hbm, far_other_hbm, probe_own_hbm, probe_other_hbm, table_hbm,
    upper, lower, grad, far, probe, table, sems, far_sems,
):
    pairs = ((probe_own_hbm, probe.at[0]), (probe_other_hbm, probe.at[1]), (table_hbm, table))
    copies = started(pairs, sems)

    def far_copies(q):
        return [
            pltpu.make_async_copy(source.at[q], far.at[m, q], far_sems.at[m, q])
            for m, source in enumerate((far_own_hbm, far_other_hbm))
        ]

    for q in range(COUNT // 2):
        for copy in far_copies(q):
            copy.start()
    grad[...] = jnp.zeros_like(grad)
    for copy in copies:
        copy.wait()

    def pair(q, carry):
        for copy in far_copies(q):
            copy.wait()
        factors = []
        for parity in range(2):
            columns = pl.ds(parity * HALF, HALF)
            rows = [change[:, 2 * q + w, :, columns].reshape(SIDE, HALF) for w in range(2)]
            factors.append(side_by_side(stacked(*rows), stacked(*rows)))
        adds = [[0.0, 0.0], [0.0, 0.0]]
        for m in range(2):
            waves = to_samples([far[m, q, side] * factors[side] for side in range(2)], table)
            for add, (real, imag) in zip(adds, waves):
                add[0] += probe[m, 0] * real + probe[m, 1] * imag
                add[1] += probe[m, 0] * imag - probe[m, 1] * real
        below = jnp.zeros((SPAN - SIDE, SIDE), jnp.float32)
        beside = jnp.zeros((SPAN, WIDTH - SIDE), jnp.float32)
        for w in range(2):
            row, col = pos[2 * q + w, 0], pos[2 * q + w, 1]
            base = pl.multiple_of(row // 8 * 8, 8)
            for part in range(2):
                placed = pltpu.roll(stacked(adds[w][part], below), row - base, 0)
                placed = pltpu.roll(side_by_side(placed, beside), col, 1)
                grad[part, pl.ds(base, SPAN), :] += placed
        return carry

    lax.fori_loop(0, COUNT // 2, pair, 0)
    for d in range(PLANE_SIZE):
        start = (d // 4) * 64 + (d % 4) * 8
        for out, half, first in ((upper, flags[1], 0), (lower, flags[3], SIDE)):
            rows = pl.ds(pl.multiple_of(start + half * 32 + first, 8), 8)
            out[d] = grad[:, rows, :]


VMEM = pl.BlockSpec(memory_space=pltpu.VMEM)
SMEM = pl.BlockSpec(memory_space=pltpu.SMEM)
HBM = pl.BlockSpec(memory_space=pltpu.HBM)
PAIRS = COUNT // 2
ALL_VMEM, MOST_VMEM, SOME_VMEM = 60, 54, 32
FAR = (PAIRS, 2, 2 * SIDE, SIDE)
SHARES = (PLANE_SIZE, COUNT, ROWS, SIDE)
DMA = pltpu.SemaphoreType.DMA


def floats(*shape):
    return jax.ShapeDtypeStruct(shape, jnp.float32)


def scratch(*shape):
    return pltpu.VMEM(shape, jnp.float32)


TABLE = pltpu.VMEM((2, 2, 2, SIDE, SIDE), jnp.bfloat16)


def call(kernel, name, in_specs, outs, scratches, operands, limit, aliases=None):
    return pl.pallas_call(
        kernel,
        out_shape=[shape for shape, _ in outs],
        in_specs=in_specs,
        out_specs=[spec for _, spec in outs],
        scratch_shapes=scratches,
        compiler_params=pltpu.CompilerParams(vmem_limit_bytes=limit * 1024 * 1024),
        cost_estimate=pl.CostEstimate(flops=0, bytes_accessed=0, transcendentals=0),
        input_output_aliases=aliases or {},
        name=name,
    )(*operands)


def body(object_field, probe_modes, amplitude, positions):
    table = jnp.asarray(tables())
    zlo, core = lax.axis_index("zlo"), lax.axis_index("core")
    y, zhi, x = (lax.axis_index(name) for name in ("y", "zhi", "x"))
    quarter = lax.rem(zlo, 4)
    lower_half = jnp.where((zlo == 15) & (core == 1), 1 - zhi, zhi)
    flags = jnp.stack([core, zhi, y * 4 + x, lower_half, quarter]).astype(jnp.int32)
    probe = probe_modes[0]

    halo = moved(object_field, along_ring(-1))
    piece = lax.dynamic_slice(probe, (core, quarter * QUARTER, 0), (1, QUARTER, SIDE))[0]
    first = moved(piece, across)
    far_own, intensity = call(
        own_kernel,
        "own",
        [SMEM] + [HBM] * 4,
        [(floats(*FAR), HBM), (floats(*SHARES), HBM)],
        [
            scratch(2, WIDTH, WIDTH),
            scratch(2, SIDE, SIDE),
            TABLE,
            scratch(*FAR),
            scratch(*SHARES),
            DMA((4,)),
            DMA((2, PAIRS)),
        ],
        (positions, object_field, halo, probe, table),
        ALL_VMEM,
    )
    (intensity,) = call(
        gate_kernel,
        "gate",
        [HBM] * 2,
        [(floats(*SHARES), HBM)],
        [],
        (intensity, first),
        MOST_VMEM,
        {0: 0},
    )
    shares = lax.all_to_all(intensity, PLANE, 0, 0)
    spread = [moved(first, move) for move in (two_on, other_core, two_on_other)]
    summed, block = call(
        collect_kernel,
        "collect",
        [VMEM] * 5,
        [(floats(COUNT, ROWS, SIDE), VMEM), (floats(2, 2, QUARTER, SIDE), VMEM)],
        [],
        (shares, first, *spread),
        SOME_VMEM,
    )
    arrived = moved(summed, other_half)
    next_block = moved(block, next_chip)
    far_other, probe_other, measured = call(
        other_kernel,
        "other",
        [SMEM] * 2 + [HBM] * 4 + [VMEM] * 2,
        [(floats(*FAR), HBM), (floats(2, SIDE, SIDE), HBM), (floats(COUNT, ROWS, SIDE), VMEM)],
        [
            scratch(2, WIDTH, WIDTH),
            scratch(COUNT, 2 * ROWS, SIDE),
            TABLE,
            scratch(2, SIDE, SIDE),
            scratch(*FAR),
            DMA((4,)),
            DMA((PAIRS + 1,)),
        ],
        (positions, flags, object_field, halo, amplitude, table, block, next_block),
        SOME_VMEM,
    )
    (change,) = call(
        change_kernel,
        "change",
        [VMEM] * 3,
        [(floats(*SHARES), VMEM)],
        [],
        (summed, arrived, measured),
        SOME_VMEM,
    )
    change = lax.all_to_all(change, PLANE, 0, 0)
    upper, lower = call(
        inverse_kernel,
        "inverse",
        [SMEM] * 2 + [VMEM] + [HBM] * 5,
        [(floats(PLANE_SIZE, 2, 8, WIDTH), VMEM)] * 2,
        [
            scratch(2, WIDTH, WIDTH),
            scratch(2, *FAR),
            scratch(2, 2, SIDE, SIDE),
            TABLE,
            DMA((3,)),
            DMA((2, PAIRS)),
        ],
        (positions, flags, change, far_own, far_other, probe, probe_other, table),
        SOME_VMEM,
    )
    gradient = upper + moved(lower, along_ring(1))
    total = jnp.sum(lax.all_to_all(gradient, PLANE, 0, 0), 0)
    own = lax.dynamic_slice_in_dim(object_field, ((y * 2 + zhi) * 4 + x) * 8, 8, 1)
    return own + 0.5 * total / MODES


def solution(mesh):
    fine = Mesh(mesh.devices.reshape(SIZES), AXES)
    tile, spec = ("zlo", "core"), ("y", "zhi", "x")
    placed = (
        P(None, tile, None),
        P(spec, None, None, None),
        P(tile, None, None),
        P(tile, None),
    )
    return jax.shard_map(
        body, mesh=fine, in_specs=placed, out_specs=P(None, tile + spec, None), check_vma=False
    )
```

```python
import math

import jax
import jax.numpy as jnp
import ml_dtypes
import numpy as np
from jax import lax
from jax.experimental import pallas as pl
from jax.experimental.pallas import tpu as pltpu
from jax.sharding import Mesh, PartitionSpec as P

AXES = ("zlo", "core", "y", "zhi", "x")
SIZES = (16, 2, 4, 2, 4)
PLANE = ("y", "x")
SIDE = 256
HALF = SIDE // 2
QUARTER = SIDE // 4
WIDTH = 512
COUNT = 4
MODES = 32
PLANE_SIZE = 16
ROWS = SIDE // PLANE_SIZE
SPAN = SIDE + 8


def pairs_of(move):
    count = math.prod(SIZES)
    pairs = []
    for source in range(count):
        place = np.unravel_index(source, SIZES)
        target = np.ravel_multi_index(move(*(int(v) for v in place)), SIZES)
        pairs.append((source, int(target)))
    return pairs


def along_ring(steps):
    def move(zlo, core, y, zhi, x):
        chip, core = divmod(((zhi * 16 + zlo) * 2 + core + steps) % 64, 2)
        return chip % 16, core, y, chip // 16, x

    return move


def other_core(zlo, core, y, zhi, x):
    return zlo, 1 - core, y, zhi, x


def other_half(zlo, core, y, zhi, x):
    return zlo, core, y, 1 - zhi, x


def next_chip(zlo, core, y, zhi, x):
    return zlo ^ 1, core, y, zhi, x


def two_on(zlo, core, y, zhi, x):
    return zlo ^ 2, core, y, zhi, x


def two_on_other(zlo, core, y, zhi, x):
    return zlo ^ 2, 1 - core, y, zhi, x


def across(zlo, core, y, zhi, x):
    chip = zhi * 16 + zlo
    chip = (chip + (8 if chip // 8 % 2 else -8)) % 32
    return chip % 16, core, y, chip // 16, x


def moved(value, move):
    return lax.ppermute(value, AXES, pairs_of(move))


def tables():
    out = np.zeros((2, 2, 2, SIDE, SIDE), ml_dtypes.bfloat16)
    for parity in range(2):
        freq = 2 * np.arange(HALF) + parity
        angle = (np.outer(freq, np.arange(HALF)) % SIDE) * (2.0 * math.pi / SIDE)
        cos, sin = np.cos(angle) / 16.0, np.sin(angle) / 16.0
        whole = np.block([[cos, sin], [-sin, cos]])
        for turned, table in enumerate((whole, whole.T)):
            high = table.astype(np.float32).astype(ml_dtypes.bfloat16)
            low = (table - high.astype(np.float64)).astype(np.float32)
            out[turned, parity, 0] = high
            out[turned, parity, 1] = low.astype(ml_dtypes.bfloat16)
    return out


def halves(value):
    high = value.astype(jnp.bfloat16)
    return high, (value - high.astype(jnp.float32)).astype(jnp.bfloat16)


def dot(a, b):
    return jnp.dot(a, b, preferred_element_type=jnp.float32)


def product(a, b):
    return dot(a[0], b[0]) + (dot(a[0], b[1]) + dot(a[1], b[0]))


def side_by_side(*parts):
    return jnp.concatenate(parts, 1)


def stacked(*parts):
    return jnp.concatenate(parts, 0)


def own_share(amp, plane):
    out_row = lax.broadcasted_iota(jnp.int32, (COUNT * ROWS, COUNT * 2 * ROWS), 0)
    in_row = lax.broadcasted_iota(jnp.int32, (COUNT * ROWS, COUNT * 2 * ROWS), 1)
    take_rows = jnp.where(in_row == 2 * out_row + plane // 8, 1.0, 0.0).astype(jnp.bfloat16)
    in_col = lax.broadcasted_iota(jnp.int32, (SIDE, SIDE), 0)
    out_col = lax.broadcasted_iota(jnp.int32, (SIDE, SIDE), 1)
    wanted = jnp.where(out_col < HALF, 2 * out_col, 2 * out_col - (SIDE - 1))
    take_cols = jnp.where(in_col == wanted, 1.0, 0.0).astype(jnp.bfloat16)
    value, total = amp.reshape(COUNT * 2 * ROWS, SIDE), 0.0
    for _ in range(3):
        part = value.astype(jnp.bfloat16)
        value = value - part.astype(jnp.float32)
        total = total + dot(dot(take_rows, part).astype(jnp.bfloat16), take_cols)
    return total.reshape(COUNT, ROWS, SIDE)


def to_frequencies(waves, table):
    parts = []
    for parity, sign in ((0, 1.0), (1, -1.0)):
        blocks = [stacked(*(part[:HALF] + sign * part[HALF:] for part in wave)) for wave in waves]
        parts.append(product(times(table, 0, parity), halves(side_by_side(*blocks))))
    outs = []
    for parity, sign in ((0, 1.0), (1, -1.0)):
        blocks = []
        for w in range(2):
            middle = w * SIDE + HALF
            for part in parts:
                block = part[:, middle - HALF : middle] + sign * part[:, middle : middle + HALF]
                blocks.append(side_by_side(block[:HALF], block[HALF:]))
        outs.append(product(halves(stacked(*blocks)), times(table, 1, parity)))
    return outs


def to_samples(far, table):
    parts = []
    for parity in range(2):
        blocks = []
        for w in range(2):
            start = w * SIDE + parity * HALF
            for side in far:
                block = side[start : start + HALF]
                blocks.append(stacked(block[:, :HALF], block[:, HALF:]))
        parts.append(product(times(table, 1, parity), halves(side_by_side(*blocks))))
    both = parts[0] + parts[1], parts[0] - parts[1]
    parts = []
    for parity in range(2):
        blocks = []
        for w in range(2):
            start = (2 * w + parity) * HALF
            for rows in both:
                block = rows[:, start : start + HALF]
                blocks.append(side_by_side(block[:HALF], block[HALF:]))
        parts.append(product(halves(stacked(*blocks)), times(table, 0, parity)))
    near, away = parts[0] + parts[1], parts[0] - parts[1]
    waves = []
    for w in range(2):
        rows = slice(w * SIDE, (w + 1) * SIDE)
        waves.append(
            (
                side_by_side(near[rows, :HALF], away[rows, :HALF]),
                side_by_side(near[rows, HALF:], away[rows, HALF:]),
            )
        )
    return waves


def times(table, turned, parity):
    return table[turned, parity, 0], table[turned, parity, 1]


def lit(probe_re, probe_im, patch_re, patch_im):
    return probe_re * patch_re - probe_im * patch_im, probe_re * patch_im + probe_im * patch_re


def windows(pos, ext, pattern):
    row, col = pos[pattern, 0], pos[pattern, 1]
    base = pl.multiple_of(row // 8 * 8, 8)
    left = lax.rem(WIDTH - col, WIDTH)
    up = lax.rem(SPAN - (row - base), SPAN)
    out = []
    for part in range(2):
        rows = pltpu.roll(ext[part, pl.ds(base, SPAN), :], left, 1)[:, :SIDE]
        out.append(pltpu.roll(rows, up, 0)[:SIDE])
    return out


def started(pairs, sems):
    copies = [pltpu.make_async_copy(*pair, sems.at[i]) for i, pair in enumerate(pairs)]
    for copy in copies:
        copy.start()
    return copies


def own_kernel(
    pos, own_hbm, halo_hbm, probe_hbm, table_hbm,
    far_hbm, intensity_hbm, ext, probe, table, far, intensity, sems, out_sems,
):
    pairs = (
        (own_hbm, ext.at[:, pl.ds(0, SIDE)]),
        (halo_hbm, ext.at[:, pl.ds(SIDE, SIDE)]),
        (probe_hbm, probe),
        (table_hbm, table),
    )
    for copy in started(pairs, sems):
        copy.wait()

    def out_copies(q):
        rows = pl.ds(2 * q, 2)
        return (
            pltpu.make_async_copy(
                intensity.at[:, rows], intensity_hbm.at[:, rows], out_sems.at[1, q]
            ),
            pltpu.make_async_copy(far.at[q], far_hbm.at[q], out_sems.at[0, q]),
        )

    def pair(q, carry):
        waves = [lit(probe[0], probe[1], *windows(pos, ext, 2 * q + w)) for w in range(2)]
        for parity, out in enumerate(to_frequencies(waves, table)):
            far[q, parity] = out
            strength = out[:, :HALF] * out[:, :HALF] + out[:, HALF:] * out[:, HALF:]
            columns = pl.ds(parity * HALF, HALF)
            for w in range(2):
                rows = strength[w * SIDE : (w + 1) * SIDE]
                intensity[:, 2 * q + w, :, columns] = rows.reshape(PLANE_SIZE, ROWS, HALF)
        for copy in out_copies(q):
            copy.start()
        return carry

    lax.fori_loop(0, PAIRS, pair, 0, unroll=True)
    for q in range(PAIRS):
        for copy in out_copies(q):
            copy.wait()


def other_kernel(
    pos, flags, own_hbm, halo_hbm, amp_hbm, table_hbm, block, next_block,
    far_hbm, probe_hbm, measured, ext, amp, table, probe, far, sems, out_sems,
):
    core, plane, quarter = flags[0], flags[2], flags[4]
    start = pl.multiple_of(lax.rem(plane, 8) * 2 * ROWS, 2 * ROWS)
    pairs = (
        (amp_hbm.at[:, pl.ds(start, 2 * ROWS)], amp),
        (table_hbm, table),
        (own_hbm, ext.at[:, pl.ds(0, SIDE)]),
        (halo_hbm, ext.at[:, pl.ds(SIDE, SIDE)]),
    )
    copies = started(pairs, sems)
    copies[0].wait()
    measured[...] = own_share(amp[...], plane)
    for copy in copies[1:]:
        copy.wait()
    for channel in range(2):
        for part in range(SIDE // QUARTER):
            apart = jnp.bitwise_xor(quarter, part)
            place = jnp.bitwise_xor(core, channel), apart // 2
            value = jnp.where(apart % 2 == 0, block[place], next_block[place])
            probe[channel, part * QUARTER : (part + 1) * QUARTER] = value
    probe_copy = pltpu.make_async_copy(probe, probe_hbm, out_sems.at[COUNT // 2])
    probe_copy.start()

    def far_copy(q):
        return pltpu.make_async_copy(far.at[q], far_hbm.at[q], out_sems.at[q])

    def pair(q, carry):
        waves = [lit(probe[0], probe[1], *windows(pos, ext, 2 * q + w)) for w in range(2)]
        for parity, out in enumerate(to_frequencies(waves, table)):
            far[q, parity] = out
        far_copy(q).start()
        return carry

    lax.fori_loop(0, COUNT // 2, pair, 0)
    for q in range(COUNT // 2):
        far_copy(q).wait()
    probe_copy.wait()


def collect_kernel(shares, first, second, crossed_first, crossed_second, summed, block):
    summed[...] = jnp.sum(shares[...], 0)
    block[0, 0] = first[...]
    block[0, 1] = second[...]
    block[1, 0] = crossed_first[...]
    block[1, 1] = crossed_second[...]


def change_kernel(summed, arrived, measured, out):
    total = summed[...] + arrived[...]
    change = measured[...] / jnp.sqrt(total + 0.05 * MODES) - 1.0
    for d in range(PLANE_SIZE):
        out[d] = change


def inverse_kernel(
    pos, flags, change, far_own_hbm, far_other_hbm, probe_own_hbm, probe_other_hbm, table_hbm,
    upper, lower, grad, far, probe, table, sems, far_sems,
):
    pairs = ((probe_own_hbm, probe.at[0]), (probe_other_hbm, probe.at[1]), (table_hbm, table))
    copies = started(pairs, sems)

    def far_copies(q):
        return [
            pltpu.make_async_copy(source.at[q], far.at[m, q], far_sems.at[m, q])
            for m, source in enumerate((far_own_hbm, far_other_hbm))
        ]

    for q in range(COUNT // 2):
        for copy in far_copies(q):
            copy.start()
    grad[...] = jnp.zeros_like(grad)
    for copy in copies:
        copy.wait()

    def pair(q, carry):
        for copy in far_copies(q):
            copy.wait()
        factors = []
        for parity in range(2):
            columns = pl.ds(parity * HALF, HALF)
            rows = [change[:, 2 * q + w, :, columns].reshape(SIDE, HALF) for w in range(2)]
            factors.append(side_by_side(stacked(*rows), stacked(*rows)))
        adds = [[0.0, 0.0], [0.0, 0.0]]
        for m in range(2):
            waves = to_samples([far[m, q, side] * factors[side] for side in range(2)], table)
            for add, (real, imag) in zip(adds, waves):
                add[0] += probe[m, 0] * real + probe[m, 1] * imag
                add[1] += probe[m, 0] * imag - probe[m, 1] * real
        below = jnp.zeros((SPAN - SIDE, SIDE), jnp.float32)
        beside = jnp.zeros((SPAN, WIDTH - SIDE), jnp.float32)
        for w in range(2):
            row, col = pos[2 * q + w, 0], pos[2 * q + w, 1]
            base = pl.multiple_of(row // 8 * 8, 8)
            for part in range(2):
                placed = pltpu.roll(stacked(adds[w][part], below), row - base, 0)
                placed = pltpu.roll(side_by_side(placed, beside), col, 1)
                grad[part, pl.ds(base, SPAN), :] += placed
        return carry

    lax.fori_loop(0, COUNT // 2, pair, 0)
    for d in range(PLANE_SIZE):
        start = (d // 4) * 64 + (d % 4) * 8
        for out, half, first in ((upper, flags[1], 0), (lower, flags[3], SIDE)):
            rows = pl.ds(pl.multiple_of(start + half * 32 + first, 8), 8)
            out[d] = grad[:, rows, :]


VMEM = pl.BlockSpec(memory_space=pltpu.VMEM)
SMEM = pl.BlockSpec(memory_space=pltpu.SMEM)
HBM = pl.BlockSpec(memory_space=pltpu.HBM)
PAIRS = COUNT // 2
ALL_VMEM, SOME_VMEM = 60, 32
FAR = (PAIRS, 2, 2 * SIDE, SIDE)
SHARES = (PLANE_SIZE, COUNT, ROWS, SIDE)
DMA = pltpu.SemaphoreType.DMA


def floats(*shape):
    return jax.ShapeDtypeStruct(shape, jnp.float32)


def scratch(*shape):
    return pltpu.VMEM(shape, jnp.float32)


TABLE = pltpu.VMEM((2, 2, 2, SIDE, SIDE), jnp.bfloat16)


def call(kernel, name, in_specs, outs, scratches, operands, limit):
    return pl.pallas_call(
        kernel,
        out_shape=[shape for shape, _ in outs],
        in_specs=in_specs,
        out_specs=[spec for _, spec in outs],
        scratch_shapes=scratches,
        compiler_params=pltpu.CompilerParams(vmem_limit_bytes=limit * 1024 * 1024),
        cost_estimate=pl.CostEstimate(flops=0, bytes_accessed=0, transcendentals=0),
        name=name,
    )(*operands)


def body(object_field, probe_modes, amplitude, positions):
    table = jnp.asarray(tables())
    zlo, core = lax.axis_index("zlo"), lax.axis_index("core")
    y, zhi, x = (lax.axis_index(name) for name in ("y", "zhi", "x"))
    quarter = lax.rem(zlo, 4)
    lower_half = jnp.where((zlo == 15) & (core == 1), 1 - zhi, zhi)
    flags = jnp.stack([core, zhi, y * 4 + x, lower_half, quarter]).astype(jnp.int32)
    probe = probe_modes[0]

    halo = moved(object_field, along_ring(-1))
    piece = lax.dynamic_slice(probe, (core, quarter * QUARTER, 0), (1, QUARTER, SIDE))[0]
    first = moved(piece, across)
    far_own, intensity = call(
        own_kernel,
        "own",
        [SMEM] + [HBM] * 4,
        [(floats(*FAR), HBM), (floats(*SHARES), HBM)],
        [
            scratch(2, WIDTH, WIDTH),
            scratch(2, SIDE, SIDE),
            TABLE,
            scratch(*FAR),
            scratch(*SHARES),
            DMA((4,)),
            DMA((2, PAIRS)),
        ],
        (positions, object_field, halo, probe, table),
        ALL_VMEM,
    )
    intensity, first = lax.optimization_barrier((intensity, first))
    shares = lax.all_to_all(intensity, PLANE, 0, 0)
    spread = [moved(first, move) for move in (two_on, other_core, two_on_other)]
    summed, block = call(
        collect_kernel,
        "collect",
        [VMEM] * 5,
        [(floats(COUNT, ROWS, SIDE), VMEM), (floats(2, 2, QUARTER, SIDE), VMEM)],
        [],
        (shares, first, *spread),
        SOME_VMEM,
    )
    arrived = moved(summed, other_half)
    next_block = moved(block, next_chip)
    far_other, probe_other, measured = call(
        other_kernel,
        "other",
        [SMEM] * 2 + [HBM] * 4 + [VMEM] * 2,
        [(floats(*FAR), HBM), (floats(2, SIDE, SIDE), HBM), (floats(COUNT, ROWS, SIDE), VMEM)],
        [
            scratch(2, WIDTH, WIDTH),
            scratch(COUNT, 2 * ROWS, SIDE),
            TABLE,
            scratch(2, SIDE, SIDE),
            scratch(*FAR),
            DMA((4,)),
            DMA((PAIRS + 1,)),
        ],
        (positions, flags, object_field, halo, amplitude, table, block, next_block),
        ALL_VMEM,
    )
    (change,) = call(
        change_kernel,
        "change",
        [VMEM] * 3,
        [(floats(*SHARES), VMEM)],
        [],
        (summed, arrived, measured),
        SOME_VMEM,
    )
    change = lax.all_to_all(change, PLANE, 0, 0)
    upper, lower = call(
        inverse_kernel,
        "inverse",
        [SMEM] * 2 + [VMEM] + [HBM] * 5,
        [(floats(PLANE_SIZE, 2, 8, WIDTH), VMEM)] * 2,
        [
            scratch(2, WIDTH, WIDTH),
            scratch(2, *FAR),
            scratch(2, 2, SIDE, SIDE),
            TABLE,
            DMA((3,)),
            DMA((2, PAIRS)),
        ],
        (positions, flags, change, far_own, far_other, probe, probe_other, table),
        SOME_VMEM,
    )
    gradient = upper + moved(lower, along_ring(1))
    total = jnp.sum(lax.all_to_all(gradient, PLANE, 0, 0), 0)
    own = lax.dynamic_slice_in_dim(object_field, ((y * 2 + zhi) * 4 + x) * 8, 8, 1)
    return own + 0.5 * total / MODES


def solution(mesh):
    fine = Mesh(mesh.devices.reshape(SIZES), AXES)
    tile, spec = ("zlo", "core"), ("y", "zhi", "x")
    placed = (
        P(None, tile, None),
        P(spec, None, None, None),
        P(tile, None, None),
        P(tile, None),
    )
    return jax.shard_map(
        body, mesh=fine, in_specs=placed, out_specs=P(None, tile + spec, None), check_vma=False
    )
```

```python
import math

import jax
import jax.numpy as jnp
import ml_dtypes
import numpy as np
from jax import lax
from jax.experimental import pallas as pl
from jax.experimental.pallas import tpu as pltpu
from jax.sharding import Mesh, PartitionSpec as P

AXES = ("zlo", "core", "y", "zhi", "x")
SIZES = (16, 2, 4, 2, 4)
PLANE = ("y", "x")
SIDE = 256
HALF = SIDE // 2
QUARTER = SIDE // 4
WIDTH = 512
COUNT = 4
MODES = 32
PLANE_SIZE = 16
ROWS = SIDE // PLANE_SIZE
SPAN = SIDE + 8


def pairs_of(move):
    count = math.prod(SIZES)
    pairs = []
    for source in range(count):
        place = np.unravel_index(source, SIZES)
        target = np.ravel_multi_index(move(*(int(v) for v in place)), SIZES)
        pairs.append((source, int(target)))
    return pairs


def along_ring(steps):
    def move(zlo, core, y, zhi, x):
        chip, core = divmod(((zhi * 16 + zlo) * 2 + core + steps) % 64, 2)
        return chip % 16, core, y, chip // 16, x

    return move


def other_core(zlo, core, y, zhi, x):
    return zlo, 1 - core, y, zhi, x


def other_half(zlo, core, y, zhi, x):
    return zlo, core, y, 1 - zhi, x


def next_chip(zlo, core, y, zhi, x):
    return zlo ^ 1, core, y, zhi, x


def two_on(zlo, core, y, zhi, x):
    return zlo ^ 2, core, y, zhi, x


def two_on_other(zlo, core, y, zhi, x):
    return zlo ^ 2, 1 - core, y, zhi, x


def across(zlo, core, y, zhi, x):
    chip = zhi * 16 + zlo
    chip = (chip + (8 if chip // 8 % 2 else -8)) % 32
    return chip % 16, core, y, chip // 16, x


def moved(value, move):
    return lax.ppermute(value, AXES, pairs_of(move))


def tables():
    out = np.zeros((2, 2, 2, SIDE, SIDE), ml_dtypes.bfloat16)
    for parity in range(2):
        freq = 2 * np.arange(HALF) + parity
        angle = (np.outer(freq, np.arange(HALF)) % SIDE) * (2.0 * math.pi / SIDE)
        cos, sin = np.cos(angle) / 16.0, np.sin(angle) / 16.0
        whole = np.block([[cos, sin], [-sin, cos]])
        for turned, table in enumerate((whole, whole.T)):
            high = table.astype(np.float32).astype(ml_dtypes.bfloat16)
            low = (table - high.astype(np.float64)).astype(np.float32)
            out[turned, parity, 0] = high
            out[turned, parity, 1] = low.astype(ml_dtypes.bfloat16)
    return out


def halves(value):
    high = value.astype(jnp.bfloat16)
    return high, (value - high.astype(jnp.float32)).astype(jnp.bfloat16)


def dot(a, b):
    return jnp.dot(a, b, preferred_element_type=jnp.float32)


def product(a, b):
    return dot(a[0], b[0]) + (dot(a[0], b[1]) + dot(a[1], b[0]))


def side_by_side(*parts):
    return jnp.concatenate(parts, 1)


def stacked(*parts):
    return jnp.concatenate(parts, 0)


def own_share(amp, plane):
    out_row = lax.broadcasted_iota(jnp.int32, (COUNT * ROWS, COUNT * 2 * ROWS), 0)
    in_row = lax.broadcasted_iota(jnp.int32, (COUNT * ROWS, COUNT * 2 * ROWS), 1)
    take_rows = jnp.where(in_row == 2 * out_row + plane // 8, 1.0, 0.0).astype(jnp.bfloat16)
    in_col = lax.broadcasted_iota(jnp.int32, (SIDE, SIDE), 0)
    out_col = lax.broadcasted_iota(jnp.int32, (SIDE, SIDE), 1)
    wanted = jnp.where(out_col < HALF, 2 * out_col, 2 * out_col - (SIDE - 1))
    take_cols = jnp.where(in_col == wanted, 1.0, 0.0).astype(jnp.bfloat16)
    value, total = amp.reshape(COUNT * 2 * ROWS, SIDE), 0.0
    for _ in range(3):
        part = value.astype(jnp.bfloat16)
        value = value - part.astype(jnp.float32)
        total = total + dot(dot(take_rows, part).astype(jnp.bfloat16), take_cols)
    return total.reshape(COUNT, ROWS, SIDE)


def to_frequencies(waves, table):
    parts = []
    for parity, sign in ((0, 1.0), (1, -1.0)):
        blocks = [stacked(*(part[:HALF] + sign * part[HALF:] for part in wave)) for wave in waves]
        parts.append(product(times(table, 0, parity), halves(side_by_side(*blocks))))
    outs = []
    for parity, sign in ((0, 1.0), (1, -1.0)):
        blocks = []
        for w in range(2):
            middle = w * SIDE + HALF
            for part in parts:
                block = part[:, middle - HALF : middle] + sign * part[:, middle : middle + HALF]
                blocks.append(side_by_side(block[:HALF], block[HALF:]))
        outs.append(product(halves(stacked(*blocks)), times(table, 1, parity)))
    return outs


def to_samples(far, table):
    parts = []
    for parity in range(2):
        blocks = []
        for w in range(2):
            start = w * SIDE + parity * HALF
            for side in far:
                block = side[start : start + HALF]
                blocks.append(stacked(block[:, :HALF], block[:, HALF:]))
        parts.append(product(times(table, 1, parity), halves(side_by_side(*blocks))))
    both = parts[0] + parts[1], parts[0] - parts[1]
    parts = []
    for parity in range(2):
        blocks = []
        for w in range(2):
            start = (2 * w + parity) * HALF
            for rows in both:
                block = rows[:, start : start + HALF]
                blocks.append(side_by_side(block[:HALF], block[HALF:]))
        parts.append(product(halves(stacked(*blocks)), times(table, 0, parity)))
    near, away = parts[0] + parts[1], parts[0] - parts[1]
    waves = []
    for w in range(2):
        rows = slice(w * SIDE, (w + 1) * SIDE)
        waves.append(
            (
                side_by_side(near[rows, :HALF], away[rows, :HALF]),
                side_by_side(near[rows, HALF:], away[rows, HALF:]),
            )
        )
    return waves


def times(table, turned, parity):
    return table[turned, parity, 0], table[turned, parity, 1]


def lit(probe_re, probe_im, patch_re, patch_im):
    return probe_re * patch_re - probe_im * patch_im, probe_re * patch_im + probe_im * patch_re


def windows(pos, ext, pattern):
    row, col = pos[pattern, 0], pos[pattern, 1]
    base = pl.multiple_of(row // 8 * 8, 8)
    left = lax.rem(WIDTH - col, WIDTH)
    up = lax.rem(SPAN - (row - base), SPAN)
    out = []
    for part in range(2):
        rows = pltpu.roll(ext[part, pl.ds(base, SPAN), :], left, 1)[:, :SIDE]
        out.append(pltpu.roll(rows, up, 0)[:SIDE])
    return out


def started(pairs, sems):
    copies = [pltpu.make_async_copy(*pair, sems.at[i]) for i, pair in enumerate(pairs)]
    for copy in copies:
        copy.start()
    return copies


def own_kernel(
    pos, own_hbm, halo_hbm, probe_hbm, table_hbm,
    far_hbm, intensity_hbm, ext, probe, table, far, intensity, sems, out_sems,
):
    pairs = (
        (own_hbm, ext.at[:, pl.ds(0, SIDE)]),
        (halo_hbm, ext.at[:, pl.ds(SIDE, SIDE)]),
        (probe_hbm, probe),
        (table_hbm, table),
    )
    for copy in started(pairs, sems):
        copy.wait()

    def out_copies(q):
        rows = pl.ds(2 * q, 2)
        return (
            pltpu.make_async_copy(
                intensity.at[:, rows], intensity_hbm.at[:, rows], out_sems.at[1, q]
            ),
            pltpu.make_async_copy(far.at[q], far_hbm.at[q], out_sems.at[0, q]),
        )

    def pair(q, carry):
        waves = [lit(probe[0], probe[1], *windows(pos, ext, 2 * q + w)) for w in range(2)]
        for parity, out in enumerate(to_frequencies(waves, table)):
            far[q, parity] = out
            strength = out[:, :HALF] * out[:, :HALF] + out[:, HALF:] * out[:, HALF:]
            columns = pl.ds(parity * HALF, HALF)
            for w in range(2):
                rows = strength[w * SIDE : (w + 1) * SIDE]
                intensity[:, 2 * q + w, :, columns] = rows.reshape(PLANE_SIZE, ROWS, HALF)
        for copy in out_copies(q):
            copy.start()
        return carry

    lax.fori_loop(0, PAIRS, pair, 0, unroll=True)
    for q in range(PAIRS):
        for copy in out_copies(q):
            copy.wait()


def share_kernel(flags, amp_hbm, measured, amp, sem):
    plane = flags[2]
    start = pl.multiple_of(lax.rem(plane, 8) * 2 * ROWS, 2 * ROWS)
    copy = pltpu.make_async_copy(amp_hbm.at[:, pl.ds(start, 2 * ROWS)], amp, sem)
    copy.start()
    copy.wait()
    measured[...] = own_share(amp[...], plane)


def other_kernel(
    pos, flags, own_hbm, halo_hbm, table_hbm, block, next_block,
    far_hbm, probe_hbm, ext, table, probe, far, sems, out_sems,
):
    core, quarter = flags[0], flags[4]
    pairs = (
        (table_hbm, table),
        (own_hbm, ext.at[:, pl.ds(0, SIDE)]),
        (halo_hbm, ext.at[:, pl.ds(SIDE, SIDE)]),
    )
    copies = started(pairs, sems)
    for channel in range(2):
        for part in range(SIDE // QUARTER):
            apart = jnp.bitwise_xor(quarter, part)
            place = jnp.bitwise_xor(core, channel), apart // 2
            value = jnp.where(apart % 2 == 0, block[place], next_block[place])
            probe[channel, part * QUARTER : (part + 1) * QUARTER] = value
    probe_copy = pltpu.make_async_copy(probe, probe_hbm, out_sems.at[COUNT // 2])
    probe_copy.start()
    for copy in copies:
        copy.wait()

    def far_copy(q):
        return pltpu.make_async_copy(far.at[q], far_hbm.at[q], out_sems.at[q])

    def pair(q, carry):
        waves = [lit(probe[0], probe[1], *windows(pos, ext, 2 * q + w)) for w in range(2)]
        for parity, out in enumerate(to_frequencies(waves, table)):
            far[q, parity] = out
        far_copy(q).start()
        return carry

    lax.fori_loop(0, COUNT // 2, pair, 0)
    for q in range(COUNT // 2):
        far_copy(q).wait()
    probe_copy.wait()


def collect_kernel(shares, first, second, crossed_first, crossed_second, summed, block):
    summed[...] = jnp.sum(shares[...], 0)
    block[0, 0] = first[...]
    block[0, 1] = second[...]
    block[1, 0] = crossed_first[...]
    block[1, 1] = crossed_second[...]


def change_kernel(summed, arrived, measured, out):
    total = summed[...] + arrived[...]
    change = measured[...] / jnp.sqrt(total + 0.05 * MODES) - 1.0
    for d in range(PLANE_SIZE):
        out[d] = change


def inverse_kernel(
    pos, flags, change, far_own_hbm, far_other_hbm, probe_own_hbm, probe_other_hbm, table_hbm,
    upper, lower, grad, far, probe, table, sems, far_sems,
):
    pairs = ((probe_own_hbm, probe.at[0]), (probe_other_hbm, probe.at[1]), (table_hbm, table))
    copies = started(pairs, sems)

    def far_copies(q):
        return [
            pltpu.make_async_copy(source.at[q], far.at[m, q], far_sems.at[m, q])
            for m, source in enumerate((far_own_hbm, far_other_hbm))
        ]

    for q in range(COUNT // 2):
        for copy in far_copies(q):
            copy.start()
    grad[...] = jnp.zeros_like(grad)
    for copy in copies:
        copy.wait()

    def pair(q, carry):
        for copy in far_copies(q):
            copy.wait()
        factors = []
        for parity in range(2):
            columns = pl.ds(parity * HALF, HALF)
            rows = [change[:, 2 * q + w, :, columns].reshape(SIDE, HALF) for w in range(2)]
            factors.append(side_by_side(stacked(*rows), stacked(*rows)))
        adds = [[0.0, 0.0], [0.0, 0.0]]
        for m in range(2):
            waves = to_samples([far[m, q, side] * factors[side] for side in range(2)], table)
            for add, (real, imag) in zip(adds, waves):
                add[0] += probe[m, 0] * real + probe[m, 1] * imag
                add[1] += probe[m, 0] * imag - probe[m, 1] * real
        below = jnp.zeros((SPAN - SIDE, SIDE), jnp.float32)
        beside = jnp.zeros((SPAN, WIDTH - SIDE), jnp.float32)
        for w in range(2):
            row, col = pos[2 * q + w, 0], pos[2 * q + w, 1]
            base = pl.multiple_of(row // 8 * 8, 8)
            for part in range(2):
                placed = pltpu.roll(stacked(adds[w][part], below), row - base, 0)
                placed = pltpu.roll(side_by_side(placed, beside), col, 1)
                grad[part, pl.ds(base, SPAN), :] += placed
        return carry

    lax.fori_loop(0, COUNT // 2, pair, 0)
    for d in range(PLANE_SIZE):
        start = (d // 4) * 64 + (d % 4) * 8
        for out, half, first in ((upper, flags[1], 0), (lower, flags[3], SIDE)):
            rows = pl.ds(pl.multiple_of(start + half * 32 + first, 8), 8)
            out[d] = grad[:, rows, :]


VMEM = pl.BlockSpec(memory_space=pltpu.VMEM)
SMEM = pl.BlockSpec(memory_space=pltpu.SMEM)
HBM = pl.BlockSpec(memory_space=pltpu.HBM)
PAIRS = COUNT // 2
ALL_VMEM, OTHER_VMEM, SOME_VMEM = 60, 52, 32
FAR = (PAIRS, 2, 2 * SIDE, SIDE)
SHARES = (PLANE_SIZE, COUNT, ROWS, SIDE)
DMA = pltpu.SemaphoreType.DMA


def floats(*shape):
    return jax.ShapeDtypeStruct(shape, jnp.float32)


def scratch(*shape):
    return pltpu.VMEM(shape, jnp.float32)


TABLE = pltpu.VMEM((2, 2, 2, SIDE, SIDE), jnp.bfloat16)


def call(kernel, name, in_specs, outs, scratches, operands, limit):
    return pl.pallas_call(
        kernel,
        out_shape=[shape for shape, _ in outs],
        in_specs=in_specs,
        out_specs=[spec for _, spec in outs],
        scratch_shapes=scratches,
        compiler_params=pltpu.CompilerParams(vmem_limit_bytes=limit * 1024 * 1024),
        cost_estimate=pl.CostEstimate(flops=0, bytes_accessed=0, transcendentals=0),
        name=name,
    )(*operands)


def body(object_field, probe_modes, amplitude, positions):
    table = jnp.asarray(tables())
    zlo, core = lax.axis_index("zlo"), lax.axis_index("core")
    y, zhi, x = (lax.axis_index(name) for name in ("y", "zhi", "x"))
    quarter = lax.rem(zlo, 4)
    lower_half = jnp.where((zlo == 15) & (core == 1), 1 - zhi, zhi)
    flags = jnp.stack([core, zhi, y * 4 + x, lower_half, quarter]).astype(jnp.int32)
    probe = probe_modes[0]

    halo = moved(object_field, along_ring(-1))
    (measured,) = call(
        share_kernel,
        "share",
        [SMEM, HBM],
        [(floats(COUNT, ROWS, SIDE), VMEM)],
        [scratch(COUNT, 2 * ROWS, SIDE), DMA(())],
        (flags, amplitude),
        SOME_VMEM,
    )
    halo, measured, flags = lax.optimization_barrier((halo, measured, flags))
    piece = lax.dynamic_slice(probe, (core, quarter * QUARTER, 0), (1, QUARTER, SIDE))[0]
    first = moved(piece, across)
    far_own, intensity = call(
        own_kernel,
        "own",
        [SMEM] + [HBM] * 4,
        [(floats(*FAR), HBM), (floats(*SHARES), HBM)],
        [
            scratch(2, WIDTH, WIDTH),
            scratch(2, SIDE, SIDE),
            TABLE,
            scratch(*FAR),
            scratch(*SHARES),
            DMA((4,)),
            DMA((2, PAIRS)),
        ],
        (positions, object_field, halo, probe, table),
        ALL_VMEM,
    )
    intensity, first = lax.optimization_barrier((intensity, first))
    shares = lax.all_to_all(intensity, PLANE, 0, 0)
    spread = [moved(first, move) for move in (two_on, other_core, two_on_other)]
    summed, block = call(
        collect_kernel,
        "collect",
        [VMEM] * 5,
        [(floats(COUNT, ROWS, SIDE), VMEM), (floats(2, 2, QUARTER, SIDE), VMEM)],
        [],
        (shares, first, *spread),
        SOME_VMEM,
    )
    arrived, block = lax.optimization_barrier((moved(summed, other_half), block))
    (change,) = call(
        change_kernel,
        "change",
        [VMEM] * 3,
        [(floats(*SHARES), VMEM)],
        [],
        (summed, arrived, measured),
        SOME_VMEM,
    )
    next_block = moved(block, next_chip)
    far_other, probe_other = call(
        other_kernel,
        "other",
        [SMEM] * 2 + [HBM] * 3 + [VMEM] * 2,
        [(floats(*FAR), HBM), (floats(2, SIDE, SIDE), HBM)],
        [
            scratch(2, WIDTH, WIDTH),
            TABLE,
            scratch(2, SIDE, SIDE),
            scratch(*FAR),
            DMA((3,)),
            DMA((PAIRS + 1,)),
        ],
        (positions, flags, object_field, halo, table, block, next_block),
        OTHER_VMEM,
    )
    change = lax.all_to_all(change, PLANE, 0, 0)
    upper, lower = call(
        inverse_kernel,
        "inverse",
        [SMEM] * 2 + [VMEM] + [HBM] * 5,
        [(floats(PLANE_SIZE, 2, 8, WIDTH), VMEM)] * 2,
        [
            scratch(2, WIDTH, WIDTH),
            scratch(2, *FAR),
            scratch(2, 2, SIDE, SIDE),
            TABLE,
            DMA((3,)),
            DMA((2, PAIRS)),
        ],
        (positions, flags, change, far_own, far_other, probe, probe_other, table),
        SOME_VMEM,
    )
    gradient = upper + moved(lower, along_ring(1))
    total = jnp.sum(lax.all_to_all(gradient, PLANE, 0, 0), 0)
    own = lax.dynamic_slice_in_dim(object_field, ((y * 2 + zhi) * 4 + x) * 8, 8, 1)
    return own + 0.5 * total / MODES


def solution(mesh):
    fine = Mesh(mesh.devices.reshape(SIZES), AXES)
    tile, spec = ("zlo", "core"), ("y", "zhi", "x")
    placed = (
        P(None, tile, None),
        P(spec, None, None, None),
        P(tile, None, None),
        P(tile, None),
    )
    return jax.shard_map(
        body, mesh=fine, in_specs=placed, out_specs=P(None, tile + spec, None), check_vma=False
    )
```

```python
import math

import jax
import jax.numpy as jnp
import ml_dtypes
import numpy as np
from jax import lax
from jax.experimental import pallas as pl
from jax.experimental.pallas import tpu as pltpu
from jax.sharding import Mesh, PartitionSpec as P

AXES = ("zlo", "core", "y", "zhi", "x")
SIZES = (16, 2, 4, 2, 4)
PLANE = ("y", "x")
SIDE = 256
HALF = SIDE // 2
QUARTER = SIDE // 4
WIDTH = 512
COUNT = 4
MODES = 32
PLANE_SIZE = 16
ROWS = SIDE // PLANE_SIZE
SPAN = SIDE + 8


def pairs_of(move):
    count = math.prod(SIZES)
    pairs = []
    for source in range(count):
        place = np.unravel_index(source, SIZES)
        target = np.ravel_multi_index(move(*(int(v) for v in place)), SIZES)
        pairs.append((source, int(target)))
    return pairs


def along_ring(steps):
    def move(zlo, core, y, zhi, x):
        chip, core = divmod(((zhi * 16 + zlo) * 2 + core + steps) % 64, 2)
        return chip % 16, core, y, chip // 16, x

    return move


def other_core(zlo, core, y, zhi, x):
    return zlo, 1 - core, y, zhi, x


def other_half(zlo, core, y, zhi, x):
    return zlo, core, y, 1 - zhi, x


def next_chip(zlo, core, y, zhi, x):
    return zlo ^ 1, core, y, zhi, x


def two_on(zlo, core, y, zhi, x):
    return zlo ^ 2, core, y, zhi, x


def two_on_other(zlo, core, y, zhi, x):
    return zlo ^ 2, 1 - core, y, zhi, x


def across(zlo, core, y, zhi, x):
    chip = zhi * 16 + zlo
    chip = (chip + (8 if chip // 8 % 2 else -8)) % 32
    return chip % 16, core, y, chip // 16, x


def moved(value, move):
    return lax.ppermute(value, AXES, pairs_of(move))


def tables():
    out = np.zeros((2, 2, 2, SIDE, SIDE), ml_dtypes.bfloat16)
    for parity in range(2):
        freq = 2 * np.arange(HALF) + parity
        angle = (np.outer(freq, np.arange(HALF)) % SIDE) * (2.0 * math.pi / SIDE)
        cos, sin = np.cos(angle) / 16.0, np.sin(angle) / 16.0
        whole = np.block([[cos, sin], [-sin, cos]])
        for turned, table in enumerate((whole, whole.T)):
            high = table.astype(np.float32).astype(ml_dtypes.bfloat16)
            low = (table - high.astype(np.float64)).astype(np.float32)
            out[turned, parity, 0] = high
            out[turned, parity, 1] = low.astype(ml_dtypes.bfloat16)
    return out


def halves(value):
    high = value.astype(jnp.bfloat16)
    return high, (value - high.astype(jnp.float32)).astype(jnp.bfloat16)


def dot(a, b):
    return jnp.dot(a, b, preferred_element_type=jnp.float32)


def product(a, b):
    return dot(a[0], b[0]) + (dot(a[0], b[1]) + dot(a[1], b[0]))


def side_by_side(*parts):
    return jnp.concatenate(parts, 1)


def stacked(*parts):
    return jnp.concatenate(parts, 0)


def own_share(amp, plane):
    out_row = lax.broadcasted_iota(jnp.int32, (COUNT * ROWS, COUNT * 2 * ROWS), 0)
    in_row = lax.broadcasted_iota(jnp.int32, (COUNT * ROWS, COUNT * 2 * ROWS), 1)
    take_rows = jnp.where(in_row == 2 * out_row + plane // 8, 1.0, 0.0).astype(jnp.bfloat16)
    in_col = lax.broadcasted_iota(jnp.int32, (SIDE, SIDE), 0)
    out_col = lax.broadcasted_iota(jnp.int32, (SIDE, SIDE), 1)
    wanted = jnp.where(out_col < HALF, 2 * out_col, 2 * out_col - (SIDE - 1))
    take_cols = jnp.where(in_col == wanted, 1.0, 0.0).astype(jnp.bfloat16)
    value, total = amp.reshape(COUNT * 2 * ROWS, SIDE), 0.0
    for _ in range(3):
        part = value.astype(jnp.bfloat16)
        value = value - part.astype(jnp.float32)
        total = total + dot(dot(take_rows, part).astype(jnp.bfloat16), take_cols)
    return total.reshape(COUNT, ROWS, SIDE)


def to_frequencies(waves, table):
    parts = []
    for parity, sign in ((0, 1.0), (1, -1.0)):
        blocks = [stacked(*(part[:HALF] + sign * part[HALF:] for part in wave)) for wave in waves]
        parts.append(product(times(table, 0, parity), halves(side_by_side(*blocks))))
    outs = []
    for parity, sign in ((0, 1.0), (1, -1.0)):
        blocks = []
        for w in range(2):
            middle = w * SIDE + HALF
            for part in parts:
                block = part[:, middle - HALF : middle] + sign * part[:, middle : middle + HALF]
                blocks.append(side_by_side(block[:HALF], block[HALF:]))
        outs.append(product(halves(stacked(*blocks)), times(table, 1, parity)))
    return outs


def to_samples(far, table):
    parts = []
    for parity in range(2):
        blocks = []
        for w in range(2):
            start = w * SIDE + parity * HALF
            for side in far:
                block = side[start : start + HALF]
                blocks.append(stacked(block[:, :HALF], block[:, HALF:]))
        parts.append(product(times(table, 1, parity), halves(side_by_side(*blocks))))
    both = parts[0] + parts[1], parts[0] - parts[1]
    parts = []
    for parity in range(2):
        blocks = []
        for w in range(2):
            start = (2 * w + parity) * HALF
            for rows in both:
                block = rows[:, start : start + HALF]
                blocks.append(side_by_side(block[:HALF], block[HALF:]))
        parts.append(product(halves(stacked(*blocks)), times(table, 0, parity)))
    near, away = parts[0] + parts[1], parts[0] - parts[1]
    waves = []
    for w in range(2):
        rows = slice(w * SIDE, (w + 1) * SIDE)
        waves.append(
            (
                side_by_side(near[rows, :HALF], away[rows, :HALF]),
                side_by_side(near[rows, HALF:], away[rows, HALF:]),
            )
        )
    return waves


def times(table, turned, parity):
    return table[turned, parity, 0], table[turned, parity, 1]


def lit(probe_re, probe_im, patch_re, patch_im):
    return probe_re * patch_re - probe_im * patch_im, probe_re * patch_im + probe_im * patch_re


def windows(pos, ext, pattern):
    row, col = pos[pattern, 0], pos[pattern, 1]
    base = pl.multiple_of(row // 8 * 8, 8)
    left = lax.rem(WIDTH - col, WIDTH)
    up = lax.rem(SPAN - (row - base), SPAN)
    out = []
    for part in range(2):
        rows = pltpu.roll(ext[part, pl.ds(base, SPAN), :], left, 1)[:, :SIDE]
        out.append(pltpu.roll(rows, up, 0)[:SIDE])
    return out


def started(pairs, sems):
    copies = [pltpu.make_async_copy(*pair, sems.at[i]) for i, pair in enumerate(pairs)]
    for copy in copies:
        copy.start()
    return copies


def own_kernel(
    pos, own_hbm, halo_hbm, probe_hbm, table_hbm,
    far_hbm, intensity_hbm, ext, probe, table, far, intensity, sems, out_sems,
):
    pairs = (
        (own_hbm, ext.at[:, pl.ds(0, SIDE)]),
        (halo_hbm, ext.at[:, pl.ds(SIDE, SIDE)]),
        (probe_hbm, probe),
        (table_hbm, table),
    )
    for copy in started(pairs, sems):
        copy.wait()

    def out_copies(q):
        rows = pl.ds(2 * q, 2)
        return (
            pltpu.make_async_copy(
                intensity.at[:, rows], intensity_hbm.at[:, rows], out_sems.at[1, q]
            ),
            pltpu.make_async_copy(far.at[q], far_hbm.at[q], out_sems.at[0, q]),
        )

    def pair(q, carry):
        waves = [lit(probe[0], probe[1], *windows(pos, ext, 2 * q + w)) for w in range(2)]
        for parity, out in enumerate(to_frequencies(waves, table)):
            far[q, parity] = out
            strength = out[:, :HALF] * out[:, :HALF] + out[:, HALF:] * out[:, HALF:]
            columns = pl.ds(parity * HALF, HALF)
            for w in range(2):
                rows = strength[w * SIDE : (w + 1) * SIDE]
                intensity[:, 2 * q + w, :, columns] = rows.reshape(PLANE_SIZE, ROWS, HALF)
        for copy in out_copies(q):
            copy.start()
        return carry

    lax.fori_loop(0, PAIRS, pair, 0, unroll=True)
    for q in range(PAIRS):
        for copy in out_copies(q):
            copy.wait()


def share_kernel(flags, amp_hbm, measured, amp, sem):
    plane = flags[2]
    start = pl.multiple_of(lax.rem(plane, 8) * 2 * ROWS, 2 * ROWS)
    copy = pltpu.make_async_copy(amp_hbm.at[:, pl.ds(start, 2 * ROWS)], amp, sem)
    copy.start()
    copy.wait()
    measured[...] = own_share(amp[...], plane)


def other_kernel(
    pos, flags, own_hbm, halo_hbm, table_hbm, block, next_block,
    far_hbm, probe_hbm, ext, table, probe, far, sems, out_sems,
):
    core, quarter = flags[0], flags[4]
    pairs = (
        (table_hbm, table),
        (own_hbm, ext.at[:, pl.ds(0, SIDE)]),
        (halo_hbm, ext.at[:, pl.ds(SIDE, SIDE)]),
    )
    copies = started(pairs, sems)
    for channel in range(2):
        for part in range(SIDE // QUARTER):
            apart = jnp.bitwise_xor(quarter, part)
            place = jnp.bitwise_xor(core, channel), apart // 2
            value = jnp.where(apart % 2 == 0, block[place], next_block[place])
            probe[channel, part * QUARTER : (part + 1) * QUARTER] = value
    probe_copy = pltpu.make_async_copy(probe, probe_hbm, out_sems.at[COUNT // 2])
    probe_copy.start()
    for copy in copies:
        copy.wait()

    def far_copy(q):
        return pltpu.make_async_copy(far.at[q], far_hbm.at[q], out_sems.at[q])

    def pair(q, carry):
        waves = [lit(probe[0], probe[1], *windows(pos, ext, 2 * q + w)) for w in range(2)]
        for parity, out in enumerate(to_frequencies(waves, table)):
            far[q, parity] = out
        far_copy(q).start()
        return carry

    lax.fori_loop(0, COUNT // 2, pair, 0)
    for q in range(COUNT // 2):
        far_copy(q).wait()
    probe_copy.wait()


def collect_kernel(shares, first, second, crossed_first, crossed_second, summed, block):
    summed[...] = jnp.sum(shares[...], 0)
    block[0, 0] = first[...]
    block[0, 1] = second[...]
    block[1, 0] = crossed_first[...]
    block[1, 1] = crossed_second[...]


def change_kernel(summed, arrived, measured, out):
    total = summed[...] + arrived[...]
    change = measured[...] / jnp.sqrt(total + 0.05 * MODES) - 1.0
    for d in range(PLANE_SIZE):
        out[d] = change


def inverse_kernel(
    pos, flags, change, far_own_hbm, far_other_hbm, probe_own_hbm, probe_other_hbm, table_hbm,
    upper, lower, grad, far, probe, table, sems, far_sems,
):
    pairs = ((probe_own_hbm, probe.at[0]), (probe_other_hbm, probe.at[1]), (table_hbm, table))
    copies = started(pairs, sems)

    def far_copies(q):
        return [
            pltpu.make_async_copy(source.at[q], far.at[m, q], far_sems.at[m, q])
            for m, source in enumerate((far_own_hbm, far_other_hbm))
        ]

    for q in range(COUNT // 2):
        for copy in far_copies(q):
            copy.start()
    grad[...] = jnp.zeros_like(grad)
    for copy in copies:
        copy.wait()

    def pair(q, carry):
        for copy in far_copies(q):
            copy.wait()
        factors = []
        for parity in range(2):
            columns = pl.ds(parity * HALF, HALF)
            rows = [change[:, 2 * q + w, :, columns].reshape(SIDE, HALF) for w in range(2)]
            factors.append(side_by_side(stacked(*rows), stacked(*rows)))
        adds = [[0.0, 0.0], [0.0, 0.0]]
        for m in range(2):
            waves = to_samples([far[m, q, side] * factors[side] for side in range(2)], table)
            for add, (real, imag) in zip(adds, waves):
                add[0] += probe[m, 0] * real + probe[m, 1] * imag
                add[1] += probe[m, 0] * imag - probe[m, 1] * real
        below = jnp.zeros((SPAN - SIDE, SIDE), jnp.float32)
        beside = jnp.zeros((SPAN, WIDTH - SIDE), jnp.float32)
        for w in range(2):
            row, col = pos[2 * q + w, 0], pos[2 * q + w, 1]
            base = pl.multiple_of(row // 8 * 8, 8)
            for part in range(2):
                placed = pltpu.roll(stacked(adds[w][part], below), row - base, 0)
                placed = pltpu.roll(side_by_side(placed, beside), col, 1)
                grad[part, pl.ds(base, SPAN), :] += placed
        return carry

    lax.fori_loop(0, COUNT // 2, pair, 0)
    for d in range(PLANE_SIZE):
        start = (d // 4) * 64 + (d % 4) * 8
        for out, half, first in ((upper, flags[1], 0), (lower, flags[3], SIDE)):
            rows = pl.ds(pl.multiple_of(start + half * 32 + first, 8), 8)
            out[d] = grad[:, rows, :]


VMEM = pl.BlockSpec(memory_space=pltpu.VMEM)
SMEM = pl.BlockSpec(memory_space=pltpu.SMEM)
HBM = pl.BlockSpec(memory_space=pltpu.HBM)
PAIRS = COUNT // 2
ALL_VMEM, OTHER_VMEM, SOME_VMEM = 60, 52, 32
FAR = (PAIRS, 2, 2 * SIDE, SIDE)
SHARES = (PLANE_SIZE, COUNT, ROWS, SIDE)
DMA = pltpu.SemaphoreType.DMA


def floats(*shape):
    return jax.ShapeDtypeStruct(shape, jnp.float32)


def scratch(*shape):
    return pltpu.VMEM(shape, jnp.float32)


TABLE = pltpu.VMEM((2, 2, 2, SIDE, SIDE), jnp.bfloat16)


def call(kernel, name, in_specs, outs, scratches, operands, limit):
    return pl.pallas_call(
        kernel,
        out_shape=[shape for shape, _ in outs],
        in_specs=in_specs,
        out_specs=[spec for _, spec in outs],
        scratch_shapes=scratches,
        compiler_params=pltpu.CompilerParams(vmem_limit_bytes=limit * 1024 * 1024),
        cost_estimate=pl.CostEstimate(flops=0, bytes_accessed=0, transcendentals=0),
        name=name,
    )(*operands)


def body(object_field, probe_modes, amplitude, positions):
    table = jnp.asarray(tables())
    zlo, core = lax.axis_index("zlo"), lax.axis_index("core")
    y, zhi, x = (lax.axis_index(name) for name in ("y", "zhi", "x"))
    quarter = lax.rem(zlo, 4)
    lower_half = jnp.where((zlo == 15) & (core == 1), 1 - zhi, zhi)
    flags = jnp.stack([core, zhi, y * 4 + x, lower_half, quarter]).astype(jnp.int32)
    probe = probe_modes[0]

    halo = moved(object_field, along_ring(-1))
    (measured,) = call(
        share_kernel,
        "share",
        [SMEM, HBM],
        [(floats(COUNT, ROWS, SIDE), VMEM)],
        [scratch(COUNT, 2 * ROWS, SIDE), DMA(())],
        (flags, amplitude),
        SOME_VMEM,
    )
    halo, measured, flags = lax.optimization_barrier((halo, measured, flags))
    piece = lax.dynamic_slice(probe, (core, quarter * QUARTER, 0), (1, QUARTER, SIDE))[0]
    first = moved(piece, across)
    far_own, intensity = call(
        own_kernel,
        "own",
        [SMEM] + [HBM] * 4,
        [(floats(*FAR), HBM), (floats(*SHARES), HBM)],
        [
            scratch(2, WIDTH, WIDTH),
            scratch(2, SIDE, SIDE),
            TABLE,
            scratch(*FAR),
            scratch(*SHARES),
            DMA((4,)),
            DMA((2, PAIRS)),
        ],
        (positions, object_field, halo, probe, table),
        ALL_VMEM,
    )
    intensity, first = lax.optimization_barrier((intensity, first))
    shares = lax.all_to_all(intensity, PLANE, 0, 0)
    spread = [moved(first, move) for move in (two_on, other_core, two_on_other)]
    summed, block = call(
        collect_kernel,
        "collect",
        [VMEM] * 5,
        [(floats(COUNT, ROWS, SIDE), VMEM), (floats(2, 2, QUARTER, SIDE), VMEM)],
        [],
        (shares, first, *spread),
        SOME_VMEM,
    )
    arrived = moved(summed, other_half)
    next_block = moved(block, next_chip)
    far_other, probe_other = call(
        other_kernel,
        "other",
        [SMEM] * 2 + [HBM] * 3 + [VMEM] * 2,
        [(floats(*FAR), HBM), (floats(2, SIDE, SIDE), HBM)],
        [
            scratch(2, WIDTH, WIDTH),
            TABLE,
            scratch(2, SIDE, SIDE),
            scratch(*FAR),
            DMA((3,)),
            DMA((PAIRS + 1,)),
        ],
        (positions, flags, object_field, halo, table, block, next_block),
        OTHER_VMEM,
    )
    arrived, far_other, probe_other = lax.optimization_barrier((arrived, far_other, probe_other))
    (change,) = call(
        change_kernel,
        "change",
        [VMEM] * 3,
        [(floats(*SHARES), VMEM)],
        [],
        (summed, arrived, measured),
        SOME_VMEM,
    )
    change = lax.all_to_all(change, PLANE, 0, 0)
    upper, lower = call(
        inverse_kernel,
        "inverse",
        [SMEM] * 2 + [VMEM] + [HBM] * 5,
        [(floats(PLANE_SIZE, 2, 8, WIDTH), VMEM)] * 2,
        [
            scratch(2, WIDTH, WIDTH),
            scratch(2, *FAR),
            scratch(2, 2, SIDE, SIDE),
            TABLE,
            DMA((3,)),
            DMA((2, PAIRS)),
        ],
        (positions, flags, change, far_own, far_other, probe, probe_other, table),
        SOME_VMEM,
    )
    gradient = upper + moved(lower, along_ring(1))
    total = jnp.sum(lax.all_to_all(gradient, PLANE, 0, 0), 0)
    own = lax.dynamic_slice_in_dim(object_field, ((y * 2 + zhi) * 4 + x) * 8, 8, 1)
    return own + 0.5 * total / MODES


def solution(mesh):
    fine = Mesh(mesh.devices.reshape(SIZES), AXES)
    tile, spec = ("zlo", "core"), ("y", "zhi", "x")
    placed = (
        P(None, tile, None),
        P(spec, None, None, None),
        P(tile, None, None),
        P(tile, None),
    )
    return jax.shard_map(
        body, mesh=fine, in_specs=placed, out_specs=P(None, tile + spec, None), check_vma=False
    )
```

```python
import math

import jax
import jax.numpy as jnp
import ml_dtypes
import numpy as np
from jax import lax
from jax.experimental import pallas as pl
from jax.experimental.pallas import tpu as pltpu
from jax.sharding import Mesh, PartitionSpec as P

AXES = ("zlo", "core", "y", "zhi", "x")
SIZES = (16, 2, 4, 2, 4)
PLANE = ("y", "x")
SIDE = 256
HALF = SIDE // 2
QUARTER = SIDE // 4
WIDTH = 512
COUNT = 4
MODES = 32
PLANE_SIZE = 16
ROWS = SIDE // PLANE_SIZE
SPAN = SIDE + 8


def pairs_of(move):
    count = math.prod(SIZES)
    pairs = []
    for source in range(count):
        place = np.unravel_index(source, SIZES)
        target = np.ravel_multi_index(move(*(int(v) for v in place)), SIZES)
        pairs.append((source, int(target)))
    return pairs


def along_ring(steps):
    def move(zlo, core, y, zhi, x):
        chip, core = divmod(((zhi * 16 + zlo) * 2 + core + steps) % 64, 2)
        return chip % 16, core, y, chip // 16, x

    return move


def other_core(zlo, core, y, zhi, x):
    return zlo, 1 - core, y, zhi, x


def other_half(zlo, core, y, zhi, x):
    return zlo, core, y, 1 - zhi, x


def next_chip(zlo, core, y, zhi, x):
    return zlo ^ 1, core, y, zhi, x


def two_on(zlo, core, y, zhi, x):
    return zlo ^ 2, core, y, zhi, x


def two_on_other(zlo, core, y, zhi, x):
    return zlo ^ 2, 1 - core, y, zhi, x


def across(zlo, core, y, zhi, x):
    chip = zhi * 16 + zlo
    chip = (chip + (8 if chip // 8 % 2 else -8)) % 32
    return chip % 16, core, y, chip // 16, x


def moved(value, move):
    return lax.ppermute(value, AXES, pairs_of(move))


def tables():
    out = np.zeros((2, 2, 2, SIDE, SIDE), ml_dtypes.bfloat16)
    for parity in range(2):
        freq = 2 * np.arange(HALF) + parity
        angle = (np.outer(freq, np.arange(HALF)) % SIDE) * (2.0 * math.pi / SIDE)
        cos, sin = np.cos(angle) / 16.0, np.sin(angle) / 16.0
        whole = np.block([[cos, sin], [-sin, cos]])
        for turned, table in enumerate((whole, whole.T)):
            high = table.astype(np.float32).astype(ml_dtypes.bfloat16)
            low = (table - high.astype(np.float64)).astype(np.float32)
            out[turned, parity, 0] = high
            out[turned, parity, 1] = low.astype(ml_dtypes.bfloat16)
    return out


def halves(value):
    high = value.astype(jnp.bfloat16)
    return high, (value - high.astype(jnp.float32)).astype(jnp.bfloat16)


def dot(a, b):
    return jnp.dot(a, b, preferred_element_type=jnp.float32)


def product(a, b):
    return dot(a[0], b[0]) + (dot(a[0], b[1]) + dot(a[1], b[0]))


def side_by_side(*parts):
    return jnp.concatenate(parts, 1)


def stacked(*parts):
    return jnp.concatenate(parts, 0)


def own_share(amp, plane):
    out_row = lax.broadcasted_iota(jnp.int32, (COUNT * ROWS, COUNT * 2 * ROWS), 0)
    in_row = lax.broadcasted_iota(jnp.int32, (COUNT * ROWS, COUNT * 2 * ROWS), 1)
    take_rows = jnp.where(in_row == 2 * out_row + plane // 8, 1.0, 0.0).astype(jnp.bfloat16)
    in_col = lax.broadcasted_iota(jnp.int32, (SIDE, SIDE), 0)
    out_col = lax.broadcasted_iota(jnp.int32, (SIDE, SIDE), 1)
    wanted = jnp.where(out_col < HALF, 2 * out_col, 2 * out_col - (SIDE - 1))
    take_cols = jnp.where(in_col == wanted, 1.0, 0.0).astype(jnp.bfloat16)
    value, total = amp.reshape(COUNT * 2 * ROWS, SIDE), 0.0
    for _ in range(3):
        part = value.astype(jnp.bfloat16)
        value = value - part.astype(jnp.float32)
        total = total + dot(dot(take_rows, part).astype(jnp.bfloat16), take_cols)
    return total.reshape(COUNT, ROWS, SIDE)


def to_frequencies(waves, table):
    parts = []
    for parity, sign in ((0, 1.0), (1, -1.0)):
        blocks = [stacked(*(part[:HALF] + sign * part[HALF:] for part in wave)) for wave in waves]
        parts.append(product(times(table, 0, parity), halves(side_by_side(*blocks))))
    outs = []
    for parity, sign in ((0, 1.0), (1, -1.0)):
        blocks = []
        for w in range(2):
            middle = w * SIDE + HALF
            for part in parts:
                block = part[:, middle - HALF : middle] + sign * part[:, middle : middle + HALF]
                blocks.append(side_by_side(block[:HALF], block[HALF:]))
        outs.append(product(halves(stacked(*blocks)), times(table, 1, parity)))
    return outs


def to_samples(far, table):
    parts = []
    for parity in range(2):
        blocks = []
        for w in range(2):
            start = w * SIDE + parity * HALF
            for side in far:
                block = side[start : start + HALF]
                blocks.append(stacked(block[:, :HALF], block[:, HALF:]))
        parts.append(product(times(table, 1, parity), halves(side_by_side(*blocks))))
    both = parts[0] + parts[1], parts[0] - parts[1]
    parts = []
    for parity in range(2):
        blocks = []
        for w in range(2):
            start = (2 * w + parity) * HALF
            for rows in both:
                block = rows[:, start : start + HALF]
                blocks.append(side_by_side(block[:HALF], block[HALF:]))
        parts.append(product(halves(stacked(*blocks)), times(table, 0, parity)))
    near, away = parts[0] + parts[1], parts[0] - parts[1]
    waves = []
    for w in range(2):
        rows = slice(w * SIDE, (w + 1) * SIDE)
        waves.append(
            (
                side_by_side(near[rows, :HALF], away[rows, :HALF]),
                side_by_side(near[rows, HALF:], away[rows, HALF:]),
            )
        )
    return waves


def times(table, turned, parity):
    return table[turned, parity, 0], table[turned, parity, 1]


def lit(probe_re, probe_im, patch_re, patch_im):
    return probe_re * patch_re - probe_im * patch_im, probe_re * patch_im + probe_im * patch_re


def windows(pos, ext, pattern):
    row, col = pos[pattern, 0], pos[pattern, 1]
    base = pl.multiple_of(row // 8 * 8, 8)
    left = lax.rem(WIDTH - col, WIDTH)
    up = lax.rem(SPAN - (row - base), SPAN)
    out = []
    for part in range(2):
        rows = pltpu.roll(ext[part, pl.ds(base, SPAN), :], left, 1)[:, :SIDE]
        out.append(pltpu.roll(rows, up, 0)[:SIDE])
    return out


def started(pairs, sems):
    copies = [pltpu.make_async_copy(*pair, sems.at[i]) for i, pair in enumerate(pairs)]
    for copy in copies:
        copy.start()
    return copies


def own_kernel(
    pos, own_hbm, halo_hbm, probe_hbm, table_hbm,
    far_hbm, intensity_hbm, ext, probe, table, far, intensity, sems, out_sems,
):
    pairs = (
        (own_hbm, ext.at[:, pl.ds(0, SIDE)]),
        (halo_hbm, ext.at[:, pl.ds(SIDE, SIDE)]),
        (probe_hbm, probe),
        (table_hbm, table),
    )
    for copy in started(pairs, sems):
        copy.wait()

    def out_copies(q):
        rows = pl.ds(2 * q, 2)
        return (
            pltpu.make_async_copy(
                intensity.at[:, rows], intensity_hbm.at[:, rows], out_sems.at[1, q]
            ),
            pltpu.make_async_copy(far.at[q], far_hbm.at[q], out_sems.at[0, q]),
        )

    def pair(q, carry):
        waves = [lit(probe[0], probe[1], *windows(pos, ext, 2 * q + w)) for w in range(2)]
        for parity, out in enumerate(to_frequencies(waves, table)):
            far[q, parity] = out
            strength = out[:, :HALF] * out[:, :HALF] + out[:, HALF:] * out[:, HALF:]
            columns = pl.ds(parity * HALF, HALF)
            for w in range(2):
                rows = strength[w * SIDE : (w + 1) * SIDE]
                intensity[:, 2 * q + w, :, columns] = rows.reshape(PLANE_SIZE, ROWS, HALF)
        for copy in out_copies(q):
            copy.start()
        return carry

    lax.fori_loop(0, PAIRS, pair, 0, unroll=True)
    for q in range(PAIRS):
        for copy in out_copies(q):
            copy.wait()


def share_kernel(flags, amp_hbm, measured, amp, sem):
    plane = flags[2]
    start = pl.multiple_of(lax.rem(plane, 8) * 2 * ROWS, 2 * ROWS)
    copy = pltpu.make_async_copy(amp_hbm.at[:, pl.ds(start, 2 * ROWS)], amp, sem)
    copy.start()
    copy.wait()
    measured[...] = own_share(amp[...], plane)


def other_kernel(
    pos, flags, own_hbm, halo_hbm, table_hbm, block, next_block,
    far_hbm, probe_hbm, ext, table, probe, far, sems, out_sems,
):
    core, quarter = flags[0], flags[4]
    pairs = (
        (table_hbm, table),
        (own_hbm, ext.at[:, pl.ds(0, SIDE)]),
        (halo_hbm, ext.at[:, pl.ds(SIDE, SIDE)]),
    )
    copies = started(pairs, sems)
    for channel in range(2):
        for part in range(SIDE // QUARTER):
            apart = jnp.bitwise_xor(quarter, part)
            place = jnp.bitwise_xor(core, channel), apart // 2
            value = jnp.where(apart % 2 == 0, block[place], next_block[place])
            probe[channel, part * QUARTER : (part + 1) * QUARTER] = value
    probe_copy = pltpu.make_async_copy(probe, probe_hbm, out_sems.at[COUNT // 2])
    probe_copy.start()
    for copy in copies:
        copy.wait()

    def far_copy(q):
        return pltpu.make_async_copy(far.at[q], far_hbm.at[q], out_sems.at[q])

    def pair(q, carry):
        waves = [lit(probe[0], probe[1], *windows(pos, ext, 2 * q + w)) for w in range(2)]
        for parity, out in enumerate(to_frequencies(waves, table)):
            far[q, parity] = out
        far_copy(q).start()
        return carry

    lax.fori_loop(0, COUNT // 2, pair, 0)
    for q in range(COUNT // 2):
        far_copy(q).wait()
    probe_copy.wait()


def collect_kernel(shares, first, second, crossed_first, crossed_second, summed, block):
    summed[...] = jnp.sum(shares[...], 0)
    block[0, 0] = first[...]
    block[0, 1] = second[...]
    block[1, 0] = crossed_first[...]
    block[1, 1] = crossed_second[...]


def change_kernel(summed, arrived, measured, out):
    total = summed[...] + arrived[...]
    change = measured[...] / jnp.sqrt(total + 0.05 * MODES) - 1.0
    for d in range(PLANE_SIZE):
        out[d] = change


def inverse_kernel(
    pos, flags, change, far_own_hbm, far_other_hbm, probe_own_hbm, probe_other_hbm, table_hbm,
    upper, lower, grad, far, probe, table, sems, far_sems,
):
    pairs = ((probe_own_hbm, probe.at[0]), (probe_other_hbm, probe.at[1]), (table_hbm, table))
    copies = started(pairs, sems)

    def far_copies(q):
        return [
            pltpu.make_async_copy(source.at[q], far.at[m, q], far_sems.at[m, q])
            for m, source in enumerate((far_own_hbm, far_other_hbm))
        ]

    for q in range(COUNT // 2):
        for copy in far_copies(q):
            copy.start()
    grad[...] = jnp.zeros_like(grad)
    for copy in copies:
        copy.wait()

    def pair(q, carry):
        for copy in far_copies(q):
            copy.wait()
        factors = []
        for parity in range(2):
            columns = pl.ds(parity * HALF, HALF)
            rows = [change[:, 2 * q + w, :, columns].reshape(SIDE, HALF) for w in range(2)]
            factors.append(side_by_side(stacked(*rows), stacked(*rows)))
        adds = [[0.0, 0.0], [0.0, 0.0]]
        for m in range(2):
            waves = to_samples([far[m, q, side] * factors[side] for side in range(2)], table)
            for add, (real, imag) in zip(adds, waves):
                add[0] += probe[m, 0] * real + probe[m, 1] * imag
                add[1] += probe[m, 0] * imag - probe[m, 1] * real
        below = jnp.zeros((SPAN - SIDE, SIDE), jnp.float32)
        beside = jnp.zeros((SPAN, WIDTH - SIDE), jnp.float32)
        for w in range(2):
            row, col = pos[2 * q + w, 0], pos[2 * q + w, 1]
            base = pl.multiple_of(row // 8 * 8, 8)
            for part in range(2):
                placed = pltpu.roll(stacked(adds[w][part], below), row - base, 0)
                placed = pltpu.roll(side_by_side(placed, beside), col, 1)
                grad[part, pl.ds(base, SPAN), :] += placed
        return carry

    lax.fori_loop(0, COUNT // 2, pair, 0)
    for d in range(PLANE_SIZE):
        start = (d // 4) * 64 + (d % 4) * 8
        for out, half, first in ((upper, flags[1], 0), (lower, flags[3], SIDE)):
            rows = pl.ds(pl.multiple_of(start + half * 32 + first, 8), 8)
            out[d] = grad[:, rows, :]


VMEM = pl.BlockSpec(memory_space=pltpu.VMEM)
SMEM = pl.BlockSpec(memory_space=pltpu.SMEM)
HBM = pl.BlockSpec(memory_space=pltpu.HBM)
PAIRS = COUNT // 2
ALL_VMEM, OTHER_VMEM, INVERSE_VMEM, SOME_VMEM = 60, 52, 46, 32
FAR = (PAIRS, 2, 2 * SIDE, SIDE)
SHARES = (PLANE_SIZE, COUNT, ROWS, SIDE)
DMA = pltpu.SemaphoreType.DMA


def floats(*shape):
    return jax.ShapeDtypeStruct(shape, jnp.float32)


def scratch(*shape):
    return pltpu.VMEM(shape, jnp.float32)


TABLE = pltpu.VMEM((2, 2, 2, SIDE, SIDE), jnp.bfloat16)


def call(kernel, name, in_specs, outs, scratches, operands, limit):
    return pl.pallas_call(
        kernel,
        out_shape=[shape for shape, _ in outs],
        in_specs=in_specs,
        out_specs=[spec for _, spec in outs],
        scratch_shapes=scratches,
        compiler_params=pltpu.CompilerParams(vmem_limit_bytes=limit * 1024 * 1024),
        cost_estimate=pl.CostEstimate(flops=0, bytes_accessed=0, transcendentals=0),
        name=name,
    )(*operands)


def body(object_field, probe_modes, amplitude, positions):
    table = jnp.asarray(tables())
    zlo, core = lax.axis_index("zlo"), lax.axis_index("core")
    y, zhi, x = (lax.axis_index(name) for name in ("y", "zhi", "x"))
    quarter = lax.rem(zlo, 4)
    lower_half = jnp.where((zlo == 15) & (core == 1), 1 - zhi, zhi)
    flags = jnp.stack([core, zhi, y * 4 + x, lower_half, quarter]).astype(jnp.int32)
    probe = probe_modes[0]

    halo = moved(object_field, along_ring(-1))
    (measured,) = call(
        share_kernel,
        "share",
        [SMEM, HBM],
        [(floats(COUNT, ROWS, SIDE), VMEM)],
        [scratch(COUNT, 2 * ROWS, SIDE), DMA(())],
        (flags, amplitude),
        SOME_VMEM,
    )
    piece = lax.dynamic_slice(probe, (core, quarter * QUARTER, 0), (1, QUARTER, SIDE))[0]
    piece, measured = lax.optimization_barrier((piece, measured))
    first = moved(piece, across)
    own = lax.dynamic_slice_in_dim(object_field, ((y * 2 + zhi) * 4 + x) * 8, 8, 1)
    halo, measured, flags, own = lax.optimization_barrier((halo, measured, flags, own))
    far_own, intensity = call(
        own_kernel,
        "own",
        [SMEM] + [HBM] * 4,
        [(floats(*FAR), HBM), (floats(*SHARES), HBM)],
        [
            scratch(2, WIDTH, WIDTH),
            scratch(2, SIDE, SIDE),
            TABLE,
            scratch(*FAR),
            scratch(*SHARES),
            DMA((4,)),
            DMA((2, PAIRS)),
        ],
        (positions, object_field, halo, probe, table),
        ALL_VMEM,
    )
    intensity, first = lax.optimization_barrier((intensity, first))
    shares = lax.all_to_all(intensity, PLANE, 0, 0)
    spread = [moved(first, move) for move in (two_on, other_core, two_on_other)]
    summed, block = call(
        collect_kernel,
        "collect",
        [VMEM] * 5,
        [(floats(COUNT, ROWS, SIDE), VMEM), (floats(2, 2, QUARTER, SIDE), VMEM)],
        [],
        (shares, first, *spread),
        SOME_VMEM,
    )
    arrived = moved(summed, other_half)
    next_block = moved(block, next_chip)
    far_other, probe_other = call(
        other_kernel,
        "other",
        [SMEM] * 2 + [HBM] * 3 + [VMEM] * 2,
        [(floats(*FAR), HBM), (floats(2, SIDE, SIDE), HBM)],
        [
            scratch(2, WIDTH, WIDTH),
            TABLE,
            scratch(2, SIDE, SIDE),
            scratch(*FAR),
            DMA((3,)),
            DMA((PAIRS + 1,)),
        ],
        (positions, flags, object_field, halo, table, block, next_block),
        OTHER_VMEM,
    )
    arrived, far_other, probe_other = lax.optimization_barrier((arrived, far_other, probe_other))
    (change,) = call(
        change_kernel,
        "change",
        [VMEM] * 3,
        [(floats(*SHARES), VMEM)],
        [],
        (summed, arrived, measured),
        SOME_VMEM,
    )
    change = lax.all_to_all(change, PLANE, 0, 0)
    upper, lower = call(
        inverse_kernel,
        "inverse",
        [SMEM] * 2 + [VMEM] + [HBM] * 5,
        [(floats(PLANE_SIZE, 2, 8, WIDTH), VMEM)] * 2,
        [
            scratch(2, WIDTH, WIDTH),
            scratch(2, *FAR),
            scratch(2, 2, SIDE, SIDE),
            TABLE,
            DMA((3,)),
            DMA((2, PAIRS)),
        ],
        (positions, flags, change, far_own, far_other, probe, probe_other, table),
        INVERSE_VMEM,
    )
    gradient = upper + moved(lower, along_ring(1))
    total = jnp.sum(lax.all_to_all(gradient, PLANE, 0, 0), 0)
    return own + 0.5 * total / MODES


def solution(mesh):
    fine = Mesh(mesh.devices.reshape(SIZES), AXES)
    tile, spec = ("zlo", "core"), ("y", "zhi", "x")
    placed = (
        P(None, tile, None),
        P(spec, None, None, None),
        P(tile, None, None),
        P(tile, None),
    )
    return jax.shard_map(
        body, mesh=fine, in_specs=placed, out_specs=P(None, tile + spec, None), check_vma=False
    )
```

```python
import math

import jax
import jax.numpy as jnp
import ml_dtypes
import numpy as np
from jax import lax
from jax.experimental import pallas as pl
from jax.experimental.pallas import tpu as pltpu
from jax.sharding import Mesh, PartitionSpec as P

AXES = ("zlo", "core", "y", "zhi", "x")
SIZES = (16, 2, 4, 2, 4)
PLANE = ("y", "x")
SIDE = 256
HALF = SIDE // 2
QUARTER = SIDE // 4
WIDTH = 512
COUNT = 4
MODES = 32
PLANE_SIZE = 16
ROWS = SIDE // PLANE_SIZE
SPAN = SIDE + 8


def pairs_of(move):
    count = math.prod(SIZES)
    pairs = []
    for source in range(count):
        place = np.unravel_index(source, SIZES)
        target = np.ravel_multi_index(move(*(int(v) for v in place)), SIZES)
        pairs.append((source, int(target)))
    return pairs


def along_ring(steps):
    def move(zlo, core, y, zhi, x):
        chip, core = divmod(((zhi * 16 + zlo) * 2 + core + steps) % 64, 2)
        return chip % 16, core, y, chip // 16, x

    return move


def other_core(zlo, core, y, zhi, x):
    return zlo, 1 - core, y, zhi, x


def other_half(zlo, core, y, zhi, x):
    return zlo, core, y, 1 - zhi, x


def next_chip(zlo, core, y, zhi, x):
    return zlo ^ 1, core, y, zhi, x


def two_on(zlo, core, y, zhi, x):
    return zlo ^ 2, core, y, zhi, x


def two_on_other(zlo, core, y, zhi, x):
    return zlo ^ 2, 1 - core, y, zhi, x


def across(zlo, core, y, zhi, x):
    chip = zhi * 16 + zlo
    chip = (chip + (8 if chip // 8 % 2 else -8)) % 32
    return chip % 16, core, y, chip // 16, x


def moved(value, move):
    return lax.ppermute(value, AXES, pairs_of(move))


def tables():
    out = np.zeros((2, 2, 2, SIDE, SIDE), ml_dtypes.bfloat16)
    for parity in range(2):
        freq = 2 * np.arange(HALF) + parity
        angle = (np.outer(freq, np.arange(HALF)) % SIDE) * (2.0 * math.pi / SIDE)
        cos, sin = np.cos(angle) / 16.0, np.sin(angle) / 16.0
        whole = np.block([[cos, sin], [-sin, cos]])
        for turned, table in enumerate((whole, whole.T)):
            high = table.astype(np.float32).astype(ml_dtypes.bfloat16)
            low = (table - high.astype(np.float64)).astype(np.float32)
            out[turned, parity, 0] = high
            out[turned, parity, 1] = low.astype(ml_dtypes.bfloat16)
    return out


def halves(value):
    high = value.astype(jnp.bfloat16)
    return high, (value - high.astype(jnp.float32)).astype(jnp.bfloat16)


def dot(a, b):
    return jnp.dot(a, b, preferred_element_type=jnp.float32)


def product(a, b):
    return dot(a[0], b[0]) + (dot(a[0], b[1]) + dot(a[1], b[0]))


def side_by_side(*parts):
    return jnp.concatenate(parts, 1)


def stacked(*parts):
    return jnp.concatenate(parts, 0)


def own_share(amp, plane):
    out_row = lax.broadcasted_iota(jnp.int32, (COUNT * ROWS, COUNT * 2 * ROWS), 0)
    in_row = lax.broadcasted_iota(jnp.int32, (COUNT * ROWS, COUNT * 2 * ROWS), 1)
    take_rows = jnp.where(in_row == 2 * out_row + plane // 8, 1.0, 0.0).astype(jnp.bfloat16)
    in_col = lax.broadcasted_iota(jnp.int32, (SIDE, SIDE), 0)
    out_col = lax.broadcasted_iota(jnp.int32, (SIDE, SIDE), 1)
    wanted = jnp.where(out_col < HALF, 2 * out_col, 2 * out_col - (SIDE - 1))
    take_cols = jnp.where(in_col == wanted, 1.0, 0.0).astype(jnp.bfloat16)
    value, total = amp.reshape(COUNT * 2 * ROWS, SIDE), 0.0
    for _ in range(3):
        part = value.astype(jnp.bfloat16)
        value = value - part.astype(jnp.float32)
        total = total + dot(dot(take_rows, part).astype(jnp.bfloat16), take_cols)
    return total.reshape(COUNT, ROWS, SIDE)


def to_frequencies(waves, table):
    parts = []
    for parity, sign in ((0, 1.0), (1, -1.0)):
        blocks = [stacked(*(part[:HALF] + sign * part[HALF:] for part in wave)) for wave in waves]
        parts.append(product(times(table, 0, parity), halves(side_by_side(*blocks))))
    outs = []
    for parity, sign in ((0, 1.0), (1, -1.0)):
        blocks = []
        for w in range(2):
            middle = w * SIDE + HALF
            for part in parts:
                block = part[:, middle - HALF : middle] + sign * part[:, middle : middle + HALF]
                blocks.append(side_by_side(block[:HALF], block[HALF:]))
        outs.append(product(halves(stacked(*blocks)), times(table, 1, parity)))
    return outs


def to_samples(far, table):
    parts = []
    for parity in range(2):
        blocks = []
        for w in range(2):
            start = w * SIDE + parity * HALF
            for side in far:
                block = side[start : start + HALF]
                blocks.append(stacked(block[:, :HALF], block[:, HALF:]))
        parts.append(product(times(table, 1, parity), halves(side_by_side(*blocks))))
    both = parts[0] + parts[1], parts[0] - parts[1]
    parts = []
    for parity in range(2):
        blocks = []
        for w in range(2):
            start = (2 * w + parity) * HALF
            for rows in both:
                block = rows[:, start : start + HALF]
                blocks.append(side_by_side(block[:HALF], block[HALF:]))
        parts.append(product(halves(stacked(*blocks)), times(table, 0, parity)))
    near, away = parts[0] + parts[1], parts[0] - parts[1]
    waves = []
    for w in range(2):
        rows = slice(w * SIDE, (w + 1) * SIDE)
        waves.append(
            (
                side_by_side(near[rows, :HALF], away[rows, :HALF]),
                side_by_side(near[rows, HALF:], away[rows, HALF:]),
            )
        )
    return waves


def times(table, turned, parity):
    return table[turned, parity, 0], table[turned, parity, 1]


def lit(probe_re, probe_im, patch_re, patch_im):
    return probe_re * patch_re - probe_im * patch_im, probe_re * patch_im + probe_im * patch_re


def windows(pos, ext, pattern):
    row, col = pos[pattern, 0], pos[pattern, 1]
    base = pl.multiple_of(row // 8 * 8, 8)
    left = lax.rem(WIDTH - col, WIDTH)
    up = lax.rem(SPAN - (row - base), SPAN)
    out = []
    for part in range(2):
        rows = pltpu.roll(ext[part, pl.ds(base, SPAN), :], left, 1)[:, :SIDE]
        out.append(pltpu.roll(rows, up, 0)[:SIDE])
    return out


def started(pairs, sems):
    copies = [pltpu.make_async_copy(*pair, sems.at[i]) for i, pair in enumerate(pairs)]
    for copy in copies:
        copy.start()
    return copies


def own_kernel(
    pos, halo, own_hbm, probe_hbm, table_hbm,
    far_hbm, intensity_hbm, ext, probe, table, far, intensity, sems, out_sems,
):
    pairs = (
        (own_hbm, ext.at[:, pl.ds(0, SIDE)]),
        (probe_hbm, probe),
        (table_hbm, table),
    )
    copies = started(pairs, sems)
    ext[:, SIDE:] = halo[...]
    for copy in copies:
        copy.wait()

    def out_copies(q):
        rows = pl.ds(2 * q, 2)
        return (
            pltpu.make_async_copy(
                intensity.at[:, rows], intensity_hbm.at[:, rows], out_sems.at[1, q]
            ),
            pltpu.make_async_copy(far.at[q], far_hbm.at[q], out_sems.at[0, q]),
        )

    def pair(q, carry):
        waves = [lit(probe[0], probe[1], *windows(pos, ext, 2 * q + w)) for w in range(2)]
        for parity, out in enumerate(to_frequencies(waves, table)):
            far[q, parity] = out
            strength = out[:, :HALF] * out[:, :HALF] + out[:, HALF:] * out[:, HALF:]
            columns = pl.ds(parity * HALF, HALF)
            for w in range(2):
                rows = strength[w * SIDE : (w + 1) * SIDE]
                intensity[:, 2 * q + w, :, columns] = rows.reshape(PLANE_SIZE, ROWS, HALF)
        for copy in out_copies(q):
            copy.start()
        return carry

    lax.fori_loop(0, PAIRS, pair, 0, unroll=True)
    for q in range(PAIRS):
        for copy in out_copies(q):
            copy.wait()


def share_kernel(flags, amp_hbm, measured, amp, sem):
    plane = flags[2]
    start = pl.multiple_of(lax.rem(plane, 8) * 2 * ROWS, 2 * ROWS)
    copy = pltpu.make_async_copy(amp_hbm.at[:, pl.ds(start, 2 * ROWS)], amp, sem)
    copy.start()
    copy.wait()
    measured[...] = own_share(amp[...], plane)


def other_kernel(
    pos, flags, own_hbm, halo_hbm, table_hbm, block, next_block,
    far_hbm, probe_hbm, ext, table, probe, far, sems, out_sems,
):
    core, quarter = flags[0], flags[4]
    pairs = (
        (table_hbm, table),
        (own_hbm, ext.at[:, pl.ds(0, SIDE)]),
        (halo_hbm, ext.at[:, pl.ds(SIDE, SIDE)]),
    )
    copies = started(pairs, sems)
    for channel in range(2):
        for part in range(SIDE // QUARTER):
            apart = jnp.bitwise_xor(quarter, part)
            place = jnp.bitwise_xor(core, channel), apart // 2
            value = jnp.where(apart % 2 == 0, block[place], next_block[place])
            probe[channel, part * QUARTER : (part + 1) * QUARTER] = value
    probe_copy = pltpu.make_async_copy(probe, probe_hbm, out_sems.at[COUNT // 2])
    probe_copy.start()
    for copy in copies:
        copy.wait()

    def far_copy(q):
        return pltpu.make_async_copy(far.at[q], far_hbm.at[q], out_sems.at[q])

    def pair(q, carry):
        waves = [lit(probe[0], probe[1], *windows(pos, ext, 2 * q + w)) for w in range(2)]
        for parity, out in enumerate(to_frequencies(waves, table)):
            far[q, parity] = out
        far_copy(q).start()
        return carry

    lax.fori_loop(0, COUNT // 2, pair, 0)
    for q in range(COUNT // 2):
        far_copy(q).wait()
    probe_copy.wait()


def collect_kernel(shares, first, second, crossed_first, crossed_second, summed, block):
    summed[...] = jnp.sum(shares[...], 0)
    block[0, 0] = first[...]
    block[0, 1] = second[...]
    block[1, 0] = crossed_first[...]
    block[1, 1] = crossed_second[...]


def change_kernel(summed, arrived, measured, out):
    total = summed[...] + arrived[...]
    change = measured[...] / jnp.sqrt(total + 0.05 * MODES) - 1.0
    for d in range(PLANE_SIZE):
        out[d] = change


def inverse_kernel(
    pos, flags, change, far_own_hbm, far_other_hbm, probe_own_hbm, probe_other_hbm, table_hbm,
    upper, lower, grad, far, probe, table, sems, far_sems,
):
    pairs = ((probe_own_hbm, probe.at[0]), (probe_other_hbm, probe.at[1]), (table_hbm, table))
    copies = started(pairs, sems)

    def far_copies(q):
        return [
            pltpu.make_async_copy(source.at[q], far.at[m, q], far_sems.at[m, q])
            for m, source in enumerate((far_own_hbm, far_other_hbm))
        ]

    for q in range(COUNT // 2):
        for copy in far_copies(q):
            copy.start()
    grad[...] = jnp.zeros_like(grad)
    for copy in copies:
        copy.wait()

    def pair(q, carry):
        for copy in far_copies(q):
            copy.wait()
        factors = []
        for parity in range(2):
            columns = pl.ds(parity * HALF, HALF)
            rows = [change[:, 2 * q + w, :, columns].reshape(SIDE, HALF) for w in range(2)]
            factors.append(side_by_side(stacked(*rows), stacked(*rows)))
        adds = [[0.0, 0.0], [0.0, 0.0]]
        for m in range(2):
            waves = to_samples([far[m, q, side] * factors[side] for side in range(2)], table)
            for add, (real, imag) in zip(adds, waves):
                add[0] += probe[m, 0] * real + probe[m, 1] * imag
                add[1] += probe[m, 0] * imag - probe[m, 1] * real
        below = jnp.zeros((SPAN - SIDE, SIDE), jnp.float32)
        beside = jnp.zeros((SPAN, WIDTH - SIDE), jnp.float32)
        for w in range(2):
            row, col = pos[2 * q + w, 0], pos[2 * q + w, 1]
            base = pl.multiple_of(row // 8 * 8, 8)
            for part in range(2):
                placed = pltpu.roll(stacked(adds[w][part], below), row - base, 0)
                placed = pltpu.roll(side_by_side(placed, beside), col, 1)
                grad[part, pl.ds(base, SPAN), :] += placed
        return carry

    lax.fori_loop(0, COUNT // 2, pair, 0)
    for d in range(PLANE_SIZE):
        start = (d // 4) * 64 + (d % 4) * 8
        for out, half, first in ((upper, flags[1], 0), (lower, flags[3], SIDE)):
            rows = pl.ds(pl.multiple_of(start + half * 32 + first, 8), 8)
            out[d] = grad[:, rows, :]


VMEM = pl.BlockSpec(memory_space=pltpu.VMEM)
SMEM = pl.BlockSpec(memory_space=pltpu.SMEM)
HBM = pl.BlockSpec(memory_space=pltpu.HBM)
PAIRS = COUNT // 2
ALL_VMEM, OTHER_VMEM, INVERSE_VMEM, SOME_VMEM = 50, 52, 46, 32
FAR = (PAIRS, 2, 2 * SIDE, SIDE)
SHARES = (PLANE_SIZE, COUNT, ROWS, SIDE)
DMA = pltpu.SemaphoreType.DMA


def floats(*shape):
    return jax.ShapeDtypeStruct(shape, jnp.float32)


def scratch(*shape):
    return pltpu.VMEM(shape, jnp.float32)


TABLE = pltpu.VMEM((2, 2, 2, SIDE, SIDE), jnp.bfloat16)


def call(kernel, name, in_specs, outs, scratches, operands, limit):
    return pl.pallas_call(
        kernel,
        out_shape=[shape for shape, _ in outs],
        in_specs=in_specs,
        out_specs=[spec for _, spec in outs],
        scratch_shapes=scratches,
        compiler_params=pltpu.CompilerParams(vmem_limit_bytes=limit * 1024 * 1024),
        cost_estimate=pl.CostEstimate(flops=0, bytes_accessed=0, transcendentals=0),
        name=name,
    )(*operands)


def body(object_field, probe_modes, amplitude, positions):
    table = jnp.asarray(tables())
    zlo, core = lax.axis_index("zlo"), lax.axis_index("core")
    y, zhi, x = (lax.axis_index(name) for name in ("y", "zhi", "x"))
    quarter = lax.rem(zlo, 4)
    lower_half = jnp.where((zlo == 15) & (core == 1), 1 - zhi, zhi)
    flags = jnp.stack([core, zhi, y * 4 + x, lower_half, quarter]).astype(jnp.int32)
    probe = probe_modes[0]

    halo = moved(object_field, along_ring(-1))
    (measured,) = call(
        share_kernel,
        "share",
        [SMEM, HBM],
        [(floats(COUNT, ROWS, SIDE), VMEM)],
        [scratch(COUNT, 2 * ROWS, SIDE), DMA(())],
        (flags, amplitude),
        SOME_VMEM,
    )
    piece = lax.dynamic_slice(probe, (core, quarter * QUARTER, 0), (1, QUARTER, SIDE))[0]
    piece, measured = lax.optimization_barrier((piece, measured))
    first = moved(piece, across)
    own = lax.dynamic_slice_in_dim(object_field, ((y * 2 + zhi) * 4 + x) * 8, 8, 1)
    halo, measured, flags, own = lax.optimization_barrier((halo, measured, flags, own))
    far_own, intensity = call(
        own_kernel,
        "own",
        [SMEM, VMEM] + [HBM] * 3,
        [(floats(*FAR), HBM), (floats(*SHARES), HBM)],
        [
            scratch(2, WIDTH, WIDTH),
            scratch(2, SIDE, SIDE),
            TABLE,
            scratch(*FAR),
            scratch(*SHARES),
            DMA((3,)),
            DMA((2, PAIRS)),
        ],
        (positions, halo, object_field, probe, table),
        ALL_VMEM,
    )
    intensity, first = lax.optimization_barrier((intensity, first))
    shares = lax.all_to_all(intensity, PLANE, 0, 0)
    spread = [moved(first, move) for move in (two_on, other_core, two_on_other)]
    summed, block = call(
        collect_kernel,
        "collect",
        [VMEM] * 5,
        [(floats(COUNT, ROWS, SIDE), VMEM), (floats(2, 2, QUARTER, SIDE), VMEM)],
        [],
        (shares, first, *spread),
        SOME_VMEM,
    )
    arrived = moved(summed, other_half)
    next_block = moved(block, next_chip)
    far_other, probe_other = call(
        other_kernel,
        "other",
        [SMEM] * 2 + [HBM] * 3 + [VMEM] * 2,
        [(floats(*FAR), HBM), (floats(2, SIDE, SIDE), HBM)],
        [
            scratch(2, WIDTH, WIDTH),
            TABLE,
            scratch(2, SIDE, SIDE),
            scratch(*FAR),
            DMA((3,)),
            DMA((PAIRS + 1,)),
        ],
        (positions, flags, object_field, halo, table, block, next_block),
        OTHER_VMEM,
    )
    arrived, far_other, probe_other = lax.optimization_barrier((arrived, far_other, probe_other))
    (change,) = call(
        change_kernel,
        "change",
        [VMEM] * 3,
        [(floats(*SHARES), VMEM)],
        [],
        (summed, arrived, measured),
        SOME_VMEM,
    )
    change = lax.all_to_all(change, PLANE, 0, 0)
    upper, lower = call(
        inverse_kernel,
        "inverse",
        [SMEM] * 2 + [VMEM] + [HBM] * 5,
        [(floats(PLANE_SIZE, 2, 8, WIDTH), VMEM)] * 2,
        [
            scratch(2, WIDTH, WIDTH),
            scratch(2, *FAR),
            scratch(2, 2, SIDE, SIDE),
            TABLE,
            DMA((3,)),
            DMA((2, PAIRS)),
        ],
        (positions, flags, change, far_own, far_other, probe, probe_other, table),
        INVERSE_VMEM,
    )
    gradient = upper + moved(lower, along_ring(1))
    total = jnp.sum(lax.all_to_all(gradient, PLANE, 0, 0), 0)
    return own + 0.5 * total / MODES


def solution(mesh):
    fine = Mesh(mesh.devices.reshape(SIZES), AXES)
    tile, spec = ("zlo", "core"), ("y", "zhi", "x")
    placed = (
        P(None, tile, None),
        P(spec, None, None, None),
        P(tile, None, None),
        P(tile, None),
    )
    return jax.shard_map(
        body, mesh=fine, in_specs=placed, out_specs=P(None, tile + spec, None), check_vma=False
    )
```

```python
import math

import jax
import jax.numpy as jnp
import ml_dtypes
import numpy as np
from jax import lax
from jax.experimental import pallas as pl
from jax.experimental.pallas import tpu as pltpu
from jax.sharding import Mesh, PartitionSpec as P

AXES = ("zlo", "core", "y", "zhi", "x")
SIZES = (16, 2, 4, 2, 4)
PLANE = ("y", "x")
SIDE = 256
HALF = SIDE // 2
QUARTER = SIDE // 4
WIDTH = 512
COUNT = 4
MODES = 32
PLANE_SIZE = 16
ROWS = SIDE // PLANE_SIZE
SPAN = SIDE + 8


def pairs_of(move):
    count = math.prod(SIZES)
    pairs = []
    for source in range(count):
        place = np.unravel_index(source, SIZES)
        target = np.ravel_multi_index(move(*(int(v) for v in place)), SIZES)
        pairs.append((source, int(target)))
    return pairs


def along_ring(steps):
    def move(zlo, core, y, zhi, x):
        chip, core = divmod(((zhi * 16 + zlo) * 2 + core + steps) % 64, 2)
        return chip % 16, core, y, chip // 16, x

    return move


def other_core(zlo, core, y, zhi, x):
    return zlo, 1 - core, y, zhi, x


def other_half(zlo, core, y, zhi, x):
    return zlo, core, y, 1 - zhi, x


def next_chip(zlo, core, y, zhi, x):
    return zlo ^ 1, core, y, zhi, x


def two_on(zlo, core, y, zhi, x):
    return zlo ^ 2, core, y, zhi, x


def two_on_other(zlo, core, y, zhi, x):
    return zlo ^ 2, 1 - core, y, zhi, x


def across(zlo, core, y, zhi, x):
    chip = zhi * 16 + zlo
    chip = (chip + (8 if chip // 8 % 2 else -8)) % 32
    return chip % 16, core, y, chip // 16, x


def moved(value, move):
    return lax.ppermute(value, AXES, pairs_of(move))


def tables():
    out = np.zeros((2, 2, 2, SIDE, SIDE), ml_dtypes.bfloat16)
    for parity in range(2):
        freq = 2 * np.arange(HALF) + parity
        angle = (np.outer(freq, np.arange(HALF)) % SIDE) * (2.0 * math.pi / SIDE)
        cos, sin = np.cos(angle) / 16.0, np.sin(angle) / 16.0
        whole = np.block([[cos, sin], [-sin, cos]])
        for turned, table in enumerate((whole, whole.T)):
            high = table.astype(np.float32).astype(ml_dtypes.bfloat16)
            low = (table - high.astype(np.float64)).astype(np.float32)
            out[turned, parity, 0] = high
            out[turned, parity, 1] = low.astype(ml_dtypes.bfloat16)
    return out


def halves(value):
    high = value.astype(jnp.bfloat16)
    return high, (value - high.astype(jnp.float32)).astype(jnp.bfloat16)


def dot(a, b):
    return jnp.dot(a, b, preferred_element_type=jnp.float32)


def product(a, b):
    return dot(a[0], b[0]) + (dot(a[0], b[1]) + dot(a[1], b[0]))


def side_by_side(*parts):
    return jnp.concatenate(parts, 1)


def stacked(*parts):
    return jnp.concatenate(parts, 0)


def own_share(amp, plane):
    out_row = lax.broadcasted_iota(jnp.int32, (COUNT * ROWS, COUNT * 2 * ROWS), 0)
    in_row = lax.broadcasted_iota(jnp.int32, (COUNT * ROWS, COUNT * 2 * ROWS), 1)
    take_rows = jnp.where(in_row == 2 * out_row + plane // 8, 1.0, 0.0).astype(jnp.bfloat16)
    in_col = lax.broadcasted_iota(jnp.int32, (SIDE, SIDE), 0)
    out_col = lax.broadcasted_iota(jnp.int32, (SIDE, SIDE), 1)
    wanted = jnp.where(out_col < HALF, 2 * out_col, 2 * out_col - (SIDE - 1))
    take_cols = jnp.where(in_col == wanted, 1.0, 0.0).astype(jnp.bfloat16)
    value, total = amp.reshape(COUNT * 2 * ROWS, SIDE), 0.0
    for _ in range(3):
        part = value.astype(jnp.bfloat16)
        value = value - part.astype(jnp.float32)
        total = total + dot(dot(take_rows, part).astype(jnp.bfloat16), take_cols)
    return total.reshape(COUNT, ROWS, SIDE)


def to_frequencies(waves, table):
    parts = []
    for parity, sign in ((0, 1.0), (1, -1.0)):
        blocks = [stacked(*(part[:HALF] + sign * part[HALF:] for part in wave)) for wave in waves]
        parts.append(product(times(table, 0, parity), halves(side_by_side(*blocks))))
    outs = []
    for parity, sign in ((0, 1.0), (1, -1.0)):
        blocks = []
        for w in range(2):
            middle = w * SIDE + HALF
            for part in parts:
                block = part[:, middle - HALF : middle] + sign * part[:, middle : middle + HALF]
                blocks.append(side_by_side(block[:HALF], block[HALF:]))
        outs.append(product(halves(stacked(*blocks)), times(table, 1, parity)))
    return outs


def to_samples(far, table):
    parts = []
    for parity in range(2):
        blocks = []
        for w in range(2):
            start = w * SIDE + parity * HALF
            for side in far:
                block = side[start : start + HALF]
                blocks.append(stacked(block[:, :HALF], block[:, HALF:]))
        parts.append(product(times(table, 1, parity), halves(side_by_side(*blocks))))
    both = parts[0] + parts[1], parts[0] - parts[1]
    parts = []
    for parity in range(2):
        blocks = []
        for w in range(2):
            start = (2 * w + parity) * HALF
            for rows in both:
                block = rows[:, start : start + HALF]
                blocks.append(side_by_side(block[:HALF], block[HALF:]))
        parts.append(product(halves(stacked(*blocks)), times(table, 0, parity)))
    near, away = parts[0] + parts[1], parts[0] - parts[1]
    waves = []
    for w in range(2):
        rows = slice(w * SIDE, (w + 1) * SIDE)
        waves.append(
            (
                side_by_side(near[rows, :HALF], away[rows, :HALF]),
                side_by_side(near[rows, HALF:], away[rows, HALF:]),
            )
        )
    return waves


def times(table, turned, parity):
    return table[turned, parity, 0], table[turned, parity, 1]


def lit(probe_re, probe_im, patch_re, patch_im):
    return probe_re * patch_re - probe_im * patch_im, probe_re * patch_im + probe_im * patch_re


def windows(pos, ext, pattern):
    row, col = pos[pattern, 0], pos[pattern, 1]
    base = pl.multiple_of(row // 8 * 8, 8)
    left = lax.rem(WIDTH - col, WIDTH)
    up = lax.rem(SPAN - (row - base), SPAN)
    out = []
    for part in range(2):
        rows = pltpu.roll(ext[part, pl.ds(base, SPAN), :], left, 1)[:, :SIDE]
        out.append(pltpu.roll(rows, up, 0)[:SIDE])
    return out


def started(pairs, sems):
    copies = [pltpu.make_async_copy(*pair, sems.at[i]) for i, pair in enumerate(pairs)]
    for copy in copies:
        copy.start()
    return copies


def own_kernel(
    pos, halo, own_hbm, probe_hbm, table_hbm,
    far_hbm, intensity_hbm, ext, probe, table, far, intensity, sems, out_sems,
):
    pairs = (
        (own_hbm, ext.at[:, pl.ds(0, SIDE)]),
        (probe_hbm, probe),
        (table_hbm, table),
    )
    copies = started(pairs, sems)
    ext[:, SIDE:] = halo[...]
    for copy in copies:
        copy.wait()

    def out_copies(q):
        rows = pl.ds(2 * q, 2)
        return (
            pltpu.make_async_copy(
                intensity.at[:, rows], intensity_hbm.at[:, rows], out_sems.at[1, q]
            ),
            pltpu.make_async_copy(far.at[q], far_hbm.at[q], out_sems.at[0, q]),
        )

    def pair(q, carry):
        waves = [lit(probe[0], probe[1], *windows(pos, ext, 2 * q + w)) for w in range(2)]
        for parity, out in enumerate(to_frequencies(waves, table)):
            far[q, parity] = out
            strength = out[:, :HALF] * out[:, :HALF] + out[:, HALF:] * out[:, HALF:]
            columns = pl.ds(parity * HALF, HALF)
            for w in range(2):
                rows = strength[w * SIDE : (w + 1) * SIDE]
                intensity[:, 2 * q + w, :, columns] = rows.reshape(PLANE_SIZE, ROWS, HALF)
        for copy in out_copies(q):
            copy.start()
        return carry

    lax.fori_loop(0, PAIRS, pair, 0, unroll=True)
    for q in range(PAIRS):
        for copy in out_copies(q):
            copy.wait()


def share_kernel(flags, amp_hbm, measured, amp, sem):
    plane = flags[2]
    start = pl.multiple_of(lax.rem(plane, 8) * 2 * ROWS, 2 * ROWS)
    copy = pltpu.make_async_copy(amp_hbm.at[:, pl.ds(start, 2 * ROWS)], amp, sem)
    copy.start()
    copy.wait()
    measured[...] = own_share(amp[...], plane)


def other_kernel(
    pos, flags, own_hbm, halo_hbm, table_hbm, block, next_block,
    far_hbm, probe_hbm, ext, table, probe, far, sems, out_sems,
):
    core, quarter = flags[0], flags[4]
    pairs = (
        (table_hbm, table),
        (own_hbm, ext.at[:, pl.ds(0, SIDE)]),
        (halo_hbm, ext.at[:, pl.ds(SIDE, SIDE)]),
    )
    copies = started(pairs, sems)
    for channel in range(2):
        for part in range(SIDE // QUARTER):
            apart = jnp.bitwise_xor(quarter, part)
            place = jnp.bitwise_xor(core, channel), apart // 2
            value = jnp.where(apart % 2 == 0, block[place], next_block[place])
            probe[channel, part * QUARTER : (part + 1) * QUARTER] = value
    probe_copy = pltpu.make_async_copy(probe, probe_hbm, out_sems.at[COUNT // 2])
    probe_copy.start()
    for copy in copies:
        copy.wait()

    def far_copy(q):
        return pltpu.make_async_copy(far.at[q], far_hbm.at[q], out_sems.at[q])

    def pair(q, carry):
        waves = [lit(probe[0], probe[1], *windows(pos, ext, 2 * q + w)) for w in range(2)]
        for parity, out in enumerate(to_frequencies(waves, table)):
            far[q, parity] = out
        far_copy(q).start()
        return carry

    lax.fori_loop(0, COUNT // 2, pair, 0)
    for q in range(COUNT // 2):
        far_copy(q).wait()
    probe_copy.wait()


def collect_kernel(shares, first, second, crossed_first, crossed_second, summed, block):
    summed[...] = jnp.sum(shares[...], 0)
    block[0, 0] = first[...]
    block[0, 1] = second[...]
    block[1, 0] = crossed_first[...]
    block[1, 1] = crossed_second[...]


def change_kernel(summed, arrived, measured, out):
    total = summed[...] + arrived[...]
    change = measured[...] / jnp.sqrt(total + 0.05 * MODES) - 1.0
    for d in range(PLANE_SIZE):
        out[d] = change


def inverse_kernel(
    pos, flags, change, far_own_hbm, far_other_hbm, probe_own_hbm, probe_other_hbm, table_hbm,
    upper, lower, grad, far, probe, table, sems, far_sems,
):
    pairs = ((probe_own_hbm, probe.at[0]), (probe_other_hbm, probe.at[1]), (table_hbm, table))
    copies = started(pairs, sems)

    def far_copies(q):
        return [
            pltpu.make_async_copy(source.at[q], far.at[m, q], far_sems.at[m, q])
            for m, source in enumerate((far_own_hbm, far_other_hbm))
        ]

    for q in range(COUNT // 2):
        for copy in far_copies(q):
            copy.start()
    grad[...] = jnp.zeros_like(grad)
    for copy in copies:
        copy.wait()

    def pair(q, carry):
        for copy in far_copies(q):
            copy.wait()
        factors = []
        for parity in range(2):
            columns = pl.ds(parity * HALF, HALF)
            rows = [change[:, 2 * q + w, :, columns].reshape(SIDE, HALF) for w in range(2)]
            factors.append(side_by_side(stacked(*rows), stacked(*rows)))
        adds = [[0.0, 0.0], [0.0, 0.0]]
        for m in range(2):
            waves = to_samples([far[m, q, side] * factors[side] for side in range(2)], table)
            for add, (real, imag) in zip(adds, waves):
                add[0] += probe[m, 0] * real + probe[m, 1] * imag
                add[1] += probe[m, 0] * imag - probe[m, 1] * real
        below = jnp.zeros((SPAN - SIDE, SIDE), jnp.float32)
        beside = jnp.zeros((SPAN, WIDTH - SIDE), jnp.float32)
        for w in range(2):
            row, col = pos[2 * q + w, 0], pos[2 * q + w, 1]
            base = pl.multiple_of(row // 8 * 8, 8)
            for part in range(2):
                placed = pltpu.roll(stacked(adds[w][part], below), row - base, 0)
                placed = pltpu.roll(side_by_side(placed, beside), col, 1)
                grad[part, pl.ds(base, SPAN), :] += placed
        return carry

    lax.fori_loop(0, COUNT // 2, pair, 0)
    for d in range(PLANE_SIZE):
        start = (d // 4) * 64 + (d % 4) * 8
        for out, half, first in ((upper, flags[1], 0), (lower, flags[3], SIDE)):
            rows = pl.ds(pl.multiple_of(start + half * 32 + first, 8), 8)
            out[d] = grad[:, rows, :]


VMEM = pl.BlockSpec(memory_space=pltpu.VMEM)
SMEM = pl.BlockSpec(memory_space=pltpu.SMEM)
HBM = pl.BlockSpec(memory_space=pltpu.HBM)
PAIRS = COUNT // 2
ALL_VMEM, OTHER_VMEM, INVERSE_VMEM, SOME_VMEM = 50, 52, 46, 32
FAR = (PAIRS, 2, 2 * SIDE, SIDE)
SHARES = (PLANE_SIZE, COUNT, ROWS, SIDE)
DMA = pltpu.SemaphoreType.DMA


def floats(*shape):
    return jax.ShapeDtypeStruct(shape, jnp.float32)


def scratch(*shape):
    return pltpu.VMEM(shape, jnp.float32)


TABLE = pltpu.VMEM((2, 2, 2, SIDE, SIDE), jnp.bfloat16)


def call(kernel, name, in_specs, outs, scratches, operands, limit):
    return pl.pallas_call(
        kernel,
        out_shape=[shape for shape, _ in outs],
        in_specs=in_specs,
        out_specs=[spec for _, spec in outs],
        scratch_shapes=scratches,
        compiler_params=pltpu.CompilerParams(vmem_limit_bytes=limit * 1024 * 1024),
        cost_estimate=pl.CostEstimate(flops=0, bytes_accessed=0, transcendentals=0),
        name=name,
    )(*operands)


def body(object_field, probe_modes, amplitude, positions):
    table = jnp.asarray(tables())
    zlo, core = lax.axis_index("zlo"), lax.axis_index("core")
    y, zhi, x = (lax.axis_index(name) for name in ("y", "zhi", "x"))
    quarter = lax.rem(zlo, 4)
    lower_half = jnp.where((zlo == 15) & (core == 1), 1 - zhi, zhi)
    flags = jnp.stack([core, zhi, y * 4 + x, lower_half, quarter]).astype(jnp.int32)
    probe = probe_modes[0]

    halo = moved(object_field, along_ring(-1))
    (measured,) = call(
        share_kernel,
        "share",
        [SMEM, HBM],
        [(floats(COUNT, ROWS, SIDE), VMEM)],
        [scratch(COUNT, 2 * ROWS, SIDE), DMA(())],
        (flags, amplitude),
        SOME_VMEM,
    )
    piece = lax.dynamic_slice(probe, (core, quarter * QUARTER, 0), (1, QUARTER, SIDE))[0]
    first = moved(piece, across)
    own = lax.dynamic_slice_in_dim(object_field, ((y * 2 + zhi) * 4 + x) * 8, 8, 1)
    halo, measured, flags, own = lax.optimization_barrier((halo, measured, flags, own))
    far_own, intensity = call(
        own_kernel,
        "own",
        [SMEM, VMEM] + [HBM] * 3,
        [(floats(*FAR), HBM), (floats(*SHARES), HBM)],
        [
            scratch(2, WIDTH, WIDTH),
            scratch(2, SIDE, SIDE),
            TABLE,
            scratch(*FAR),
            scratch(*SHARES),
            DMA((3,)),
            DMA((2, PAIRS)),
        ],
        (positions, halo, object_field, probe, table),
        ALL_VMEM,
    )
    intensity, first = lax.optimization_barrier((intensity, first))
    shares = lax.all_to_all(intensity, PLANE, 0, 0)
    spread = [moved(first, move) for move in (two_on, other_core, two_on_other)]
    summed, block = call(
        collect_kernel,
        "collect",
        [VMEM] * 5,
        [(floats(COUNT, ROWS, SIDE), VMEM), (floats(2, 2, QUARTER, SIDE), VMEM)],
        [],
        (shares, first, *spread),
        SOME_VMEM,
    )
    arrived = moved(summed, other_half)
    next_block = moved(block, next_chip)
    far_other, probe_other = call(
        other_kernel,
        "other",
        [SMEM] * 2 + [HBM] * 3 + [VMEM] * 2,
        [(floats(*FAR), HBM), (floats(2, SIDE, SIDE), HBM)],
        [
            scratch(2, WIDTH, WIDTH),
            TABLE,
            scratch(2, SIDE, SIDE),
            scratch(*FAR),
            DMA((3,)),
            DMA((PAIRS + 1,)),
        ],
        (positions, flags, object_field, halo, table, block, next_block),
        OTHER_VMEM,
    )
    arrived, far_other, probe_other = lax.optimization_barrier((arrived, far_other, probe_other))
    (change,) = call(
        change_kernel,
        "change",
        [VMEM] * 3,
        [(floats(*SHARES), VMEM)],
        [],
        (summed, arrived, measured),
        SOME_VMEM,
    )
    change = lax.all_to_all(change, PLANE, 0, 0)
    upper, lower = call(
        inverse_kernel,
        "inverse",
        [SMEM] * 2 + [VMEM] + [HBM] * 5,
        [(floats(PLANE_SIZE, 2, 8, WIDTH), VMEM)] * 2,
        [
            scratch(2, WIDTH, WIDTH),
            scratch(2, *FAR),
            scratch(2, 2, SIDE, SIDE),
            TABLE,
            DMA((3,)),
            DMA((2, PAIRS)),
        ],
        (positions, flags, change, far_own, far_other, probe, probe_other, table),
        INVERSE_VMEM,
    )
    gradient = upper + moved(lower, along_ring(1))
    total = jnp.sum(lax.all_to_all(gradient, PLANE, 0, 0), 0)
    return own + 0.5 * total / MODES


def solution(mesh):
    fine = Mesh(mesh.devices.reshape(SIZES), AXES)
    tile, spec = ("zlo", "core"), ("y", "zhi", "x")
    placed = (
        P(None, tile, None),
        P(spec, None, None, None),
        P(tile, None, None),
        P(tile, None),
    )
    return jax.shard_map(
        body, mesh=fine, in_specs=placed, out_specs=P(None, tile + spec, None), check_vma=False
    )
```
